32 devices in a mesh: node: 16 (over z, y, x), edge: 2 (over core).
Axes of the slice: x: 2, y: 2, z: 4, core: 2. Of those that a mesh axis runs over, the one named last changes fastest.
Arguments:
- embedding: bfloat16 [128, 128, 512], P('node'), may hold values from -6 to 6
- send_list: int32 [2, 16, 16], P('edge', 'node'), may hold values from -1 to 7, as said below
- edge_ends: int32 [2, 65536], P(None, ('node', 'edge')), may hold values from 0 to 16383, as said below
- pair_index: int32 [65536], P(('node', 'edge')), may hold values from 0 to 16383, as said below
- w_first: bfloat16 [1024, 512], replicated, may hold values from -0.1875 to 0.1875
- b_first: float32 [512], replicated, may hold values from -3 to 3
- w_second: bfloat16 [512], replicated, may hold values from -0.25 to 0.25
Outputs:
- edge_score: float32 [65536], P(('node', 'edge'))
- pair_cost: float32 [16384], P(('node', 'edge'))
The draws below stay inside these ranges and needn't reach their ends.
Inputs may be any that keep to these rules, and one draw needn't show every extreme that they name: Each entry is -1 or a block index of the sending node index; send_list[e, k, k] is never -1. `edge_ends`: node ids; most ends lie in a block that the send list delivers to the edge's node group and edge index. `pair_index`: an edge of node group j has a pair in j * 1024 to (j + 1) * 1024 - 1.
All inputs are finite; a program needn't handle non-finite values.
Results may differ from the reference program's by a relative error of at most 0.0003.
Values may be sent and summed in bfloat16 or wider, within the bound.
No kernel may reach another device: no remote copies, remote signals or barrier semaphores. Data moves between devices by JAX's collectives and lax.ppermute only.
A program may use at most 64 MiB of HBM per device.

```python
import jax
import jax.numpy as jnp
from jax import lax

F = 512
HID = 512
BLOCK = 128
NB_DEV = 8
E_DEV = 2048
PAIRS_ROW = 1024
NODE_BLOCKS = 128
NODES = 16384
EDGES = 65536
PAIRS = 16384
N_NODE = 16
N_EDGE = 2


def routing(key):
    first_key, second_key = jax.random.split(jax.random.fold_in(key, 11), 2)
    shape_all = (N_EDGE, N_NODE, N_NODE)
    living = jax.random.randint(first_key, shape_all, 0, 5) < 3
    chosen = jax.random.randint(second_key, shape_all, 0, NB_DEV)
    source = jnp.arange(N_NODE)[None, :, None]
    target = jnp.arange(N_NODE)[None, None, :]
    diagonal = source == target
    chosen = jnp.where(diagonal & (source == 0), 0, chosen)
    chosen = jnp.where(diagonal & (source == N_NODE - 1), NB_DEV - 1, chosen)
    living = living | diagonal
    return jnp.where(living, chosen, -1).astype(jnp.int32)


def draw_send_list(key, part):
    return routing(key)


def draw_edge_ends(key, part):
    lists_all = routing(key)
    key_source, key_row, key_any, key_pick = jax.random.split(jax.random.fold_in(key, 23), 4)
    device = jnp.arange(EDGES) // E_DEV
    group = jnp.broadcast_to(device // N_EDGE, (2, EDGES))
    edge_pos = jnp.broadcast_to(device % N_EDGE, (2, EDGES))
    source = jax.random.randint(key_source, (2, EDGES), 0, N_NODE)
    block_here = lists_all[edge_pos, source, group]
    source = jnp.where(block_here >= 0, source, group)
    block_here = lists_all[edge_pos, source, group]
    row_here = jax.random.randint(key_row, (2, EDGES), 0, BLOCK)
    delivered = (source * NB_DEV + block_here) * BLOCK + row_here
    any_ids = jax.random.randint(key_any, (2, EDGES), 0, NODES)
    picker = jax.random.randint(key_pick, (2, EDGES), 0, 10) < 9
    node_ids = jnp.where(picker, delivered, any_ids)
    own_block = (group * NB_DEV + lists_all[edge_pos, group, group]) * BLOCK
    leading = (jnp.arange(EDGES) % E_DEV == 0)[None, :]
    fixed_ends = jnp.concatenate([own_block[:1], own_block[1:] + BLOCK - 1], axis=0)
    node_ids = jnp.where(leading, fixed_ends, node_ids)
    return node_ids.astype(jnp.int32)


def draw_pair_index(key, part):
    device = jnp.arange(EDGES) // E_DEV
    group = device // N_EDGE
    offset = jax.random.randint(jax.random.fold_in(key, 37), (EDGES,), 0, PAIRS_ROW)
    position = jnp.arange(EDGES) % E_DEV
    offset = jnp.where(position == 0, 0, offset)
    offset = jnp.where(position == 1, PAIRS_ROW - 1, offset)
    return (group * PAIRS_ROW + offset).astype(jnp.int32)


def level_of(key, dims, pieces, least, high):
    factor_of = 1.0
    for dim, parts in pieces:
        steps = jax.random.uniform(jax.random.fold_in(jax.random.fold_in(key, 6), dim), (parts,), jnp.float32, least / len(pieces), high / len(pieces))
        factor_of = factor_of * jnp.repeat(jnp.exp(steps), dims[dim] // parts).reshape((-1,) + (1,) * (len(dims) - 1 - dim))
    return factor_of


def centred(stream_key, dims, scale, limit, cuts=(), kind=jnp.bfloat16):
    drawn = jax.random.normal(stream_key, dims, jnp.float32) * scale
    if len(cuts) > 0:
        drawn = level_of(stream_key, dims, cuts, -0.22, 0.18) * drawn
    return jnp.clip(drawn, min=-limit, max=limit).astype(kind)


def setup_inputs(seed: int = 0) -> dict:
    seeds = jax.random.split(jax.random.key(seed), 8)
    embedding = centred(seeds[0], (NODE_BLOCKS, BLOCK, F), 1.0, 6.0, ((0, 16),))
    send_list = draw_send_list(jax.random.fold_in(seeds[7], 71), 0)
    edge_ends = draw_edge_ends(jax.random.fold_in(seeds[7], 71), 0)
    pair_index = draw_pair_index(jax.random.fold_in(seeds[7], 71), 0)
    w_first = centred(seeds[4], (2 * F, HID), (2 * F) ** -0.5, 0.1875)
    b_first = centred(seeds[5], (HID,), 0.5, 3.0, (), jnp.float32)
    w_second = centred(seeds[6], (HID,), HID ** -0.5, 0.25)
    return dict(embedding=embedding, send_list=send_list, edge_ends=edge_ends, pair_index=pair_index, w_first=w_first, b_first=b_first, w_second=w_second)


def reference(embedding, send_list, edge_ends, pair_index, w_first, b_first, w_second):
    flat_rows = embedding.reshape(NODES, F)
    upper = w_first[:F]
    bottom = w_first[F:]
    w_out = w_second.astype(jnp.float32)

    def device_scores(device):
        group = device // N_EDGE
        edge_pos = device % N_EDGE
        node_ids = lax.dynamic_slice(edge_ends, (jnp.int32(0), (device * E_DEV).astype(jnp.int32)), (2, E_DEV))
        block_ids = node_ids // BLOCK
        source = block_ids // NB_DEV
        lists_here = lax.dynamic_index_in_dim(send_list, edge_pos, 0, False)
        column = lax.dynamic_index_in_dim(lists_here, group, 1, False)
        present = jnp.take(column, source) == block_ids % NB_DEV
        end_rows = jnp.take(flat_rows, node_ids, axis=0)
        end_rows = jnp.where(present[..., None], end_rows, jnp.zeros_like(end_rows))
        preact = jnp.dot(end_rows[0], upper, preferred_element_type=jnp.float32)
        preact = preact + jnp.dot(end_rows[1], bottom, preferred_element_type=jnp.float32) + b_first
        hidden = jax.nn.gelu(preact, approximate=True)
        return jnp.dot(hidden, w_out, precision=lax.Precision.HIGHEST)

    scores = lax.map(device_scores, jnp.arange(EDGES // E_DEV, dtype=jnp.int32))
    edge_score = scores.reshape(EDGES)
    pair_cost = jnp.zeros((PAIRS,), jnp.float32).at[pair_index].add(edge_score)
    return edge_score, pair_cost
```

```python
import functools

import jax
import jax.numpy as jnp
from jax import lax
from jax.experimental import pallas as pl
from jax.experimental.pallas import tpu as pltpu
from jax.sharding import PartitionSpec as P

PAIRS_ROW = 1024
LANES = 128
LEAD = 8


def scorer(
    edge_total,
    parts,
    rows_ref,
    offsets_hbm,
    pair_ref,
    weight_ref,
    bias_ref,
    out_weight_ref,
    score_ref,
    pooled_ref,
    first_table,
    second_table,
    terms,
    offsets,
    offsets_sem,
):
    row_total = rows_ref.shape[0]
    hidden_width = parts * LANES
    offsets_copy = pltpu.make_async_copy(offsets_hbm, offsets, offsets_sem)
    offsets_copy.start()

    tile = 256
    bias = bias_ref[...]
    last = LEAD + row_total * parts
    first_table[pl.ds(last, 8), :] = bias
    second_table[pl.ds(last, 8), :] = jnp.zeros((8, LANES), jnp.float32)

    def project(step, carry):
        start = pl.multiple_of(step * tile, tile)
        rows = rows_ref[pl.ds(start, tile), :]
        shares = jnp.dot(rows, weight_ref[...], preferred_element_type=jnp.float32)
        for part in range(parts):
            lower = shares[:, part * LANES : (part + 1) * LANES]
            upper = shares[:, hidden_width + part * LANES : hidden_width + (part + 1) * LANES]
            at = pl.ds(LEAD + start * parts + part, tile, stride=parts)
            first_table[at, :] = lower + bias[part : part + 1, :]
            second_table[at, :] = upper
        return carry

    lax.fori_loop(0, row_total // tile, project, 0)
    offsets_copy.wait()

    out_weight = out_weight_ref[...]
    early = lax.broadcasted_iota(jnp.int32, (8, LANES), 0) < parts
    group = 16

    def score_group(step, carry):
        for pair in range(group // 2):
            edge = step * group + 2 * pair
            first = jnp.where(
                early,
                first_table[pl.ds(offsets[edge], 8), :],
                first_table[pl.ds(offsets[edge + 1], 8), :],
            )
            second = jnp.where(
                early,
                second_table[pl.ds(offsets[edge_total + edge], 8), :],
                second_table[pl.ds(offsets[edge_total + edge + 1], 8), :],
            )
            x = first + second
            inner = x * (0.7978845608028654 + (0.7978845608028654 * 0.044715) * (x * x))
            weighted = x * out_weight
            terms[pl.ds(pl.multiple_of(edge * parts, 8), 8), :] = weighted + weighted * jnp.tanh(inner)
        return carry

    lax.fori_loop(0, edge_total // group, score_group, 0)

    sums = terms[pl.ds(0, edge_total, stride=parts), :]
    for part in range(1, parts):
        sums = sums + terms[pl.ds(part, edge_total, stride=parts), :]
    ones = jnp.ones((8, LANES), jnp.float32)
    scores = lax.dot_general(
        ones, sums, (((1,), (1,)), ((), ())), precision=lax.Precision.HIGHEST, preferred_element_type=jnp.float32
    )
    score_ref[...] = scores[0:1, :]

    pair = pair_ref[...]
    pair_rows = PAIRS_ROW // LANES
    high = lax.broadcasted_iota(jnp.int32, (pair_rows, edge_total), 0) == pair // LANES
    low = lax.broadcasted_iota(jnp.int32, (LANES, edge_total), 0) == pair % LANES
    spread = jnp.where(high, scores[:pair_rows], 0.0)
    pooled_ref[...] = lax.dot_general(
        spread,
        low.astype(jnp.float32),
        (((1,), (1,)), ((), ())),
        precision=lax.Precision.HIGHEST,
        preferred_element_type=jnp.float32,
    )


def body(embedding, send_list, edge_ends, pair_index, w_first, b_first, w_second):
    node_count = lax.axis_size("node")
    node_self = lax.axis_index("node")
    blocks_here, block_rows, feature_width = embedding.shape
    hidden_width = w_first.shape[1]
    parts = hidden_width // LANES
    edge_total = edge_ends.shape[1]
    row_total = node_count * block_rows

    wanted = send_list[0, 0]
    picked = jnp.take(embedding, jnp.clip(wanted, 0, blocks_here - 1), axis=0)
    arrived = lax.all_to_all(picked, "node", split_axis=0, concat_axis=0, tiled=True)
    rows = arrived.reshape(row_total, feature_width)

    lists = lax.all_gather(wanted, "node")
    block_here = lax.dynamic_index_in_dim(lists, node_self, 1, False)
    target = edge_ends // block_rows
    source = target // blocks_here
    sources = jnp.arange(node_count, dtype=jnp.int32)
    delivered = jnp.sum(jnp.where(source[..., None] == sources, block_here, 0), axis=-1)
    row = jnp.where(delivered == target % blocks_here, source * block_rows + edge_ends % block_rows, row_total)
    second_of_two = jnp.arange(edge_total, dtype=jnp.int32) % 2
    offsets = (LEAD + row * parts - second_of_two * parts).reshape(2 * edge_total)

    weight = jnp.concatenate([w_first[:feature_width], w_first[feature_width:]], axis=1)
    bias = jnp.tile(b_first.reshape(parts, LANES), (8 // parts, 1))
    out_weight = jnp.tile(0.5 * w_second.astype(jnp.float32).reshape(parts, LANES), (8 // parts, 1))
    pair_here = (pair_index - node_self * PAIRS_ROW).reshape(1, edge_total)

    table = pltpu.VMEM((LEAD + row_total * parts + 8, LANES), jnp.float32)
    vmem = pl.BlockSpec(memory_space=pltpu.VMEM)
    scores, pooled = pl.pallas_call(
        functools.partial(scorer, edge_total, parts),
        out_shape=(
            jax.ShapeDtypeStruct((1, edge_total), jnp.float32),
            jax.ShapeDtypeStruct((PAIRS_ROW // LANES, LANES), jnp.float32),
        ),
        in_specs=[vmem, pl.BlockSpec(memory_space=pl.ANY), vmem, vmem, vmem, vmem],
        out_specs=(vmem, vmem),
        scratch_shapes=[
            table,
            table,
            pltpu.VMEM((edge_total * parts, LANES), jnp.float32),
            pltpu.SMEM((2 * edge_total,), jnp.int32),
            pltpu.SemaphoreType.DMA,
        ],
        compiler_params=pltpu.CompilerParams(vmem_limit_bytes=56 * 2**20),
    )(rows, offsets, pair_here, weight, bias, out_weight)
    edge_score = scores.reshape(edge_total)
    pair_cost = lax.psum_scatter(pooled.reshape(PAIRS_ROW), "edge", scatter_dimension=0, tiled=True)
    return (edge_score, pair_cost)


def solution(mesh):
    return jax.shard_map(
        body,
        mesh=mesh,
        in_specs=(
            P("node", None, None),
            P("edge", "node", None),
            P(None, ("node", "edge")),
            P(("node", "edge")),
            P(),
            P(),
            P(),
        ),
        out_specs=(P(("node", "edge")), P(("node", "edge"))),
        check_vma=False,
    )
```

```python
import functools

import jax
import jax.numpy as jnp
from jax import lax
from jax.experimental import pallas as pl
from jax.experimental.pallas import tpu as pltpu
from jax.sharding import PartitionSpec as P

PAIRS_ROW = 1024
LANES = 128
LEAD = 8
LABEL_ROWS = 8
GELU_A = 0.7978845608028654
GELU_B = GELU_A * 0.044715


def bits(power_of_two):
    return power_of_two.bit_length() - 1


def pick(wanted_ref, embedding_ref, sent_ref, labels, block_sem, label_sem):
    node_count = sent_ref.shape[0]
    blocks_here, block_rows, feature_width = embedding_ref.shape
    groups = feature_width // LANES
    body_rows = groups * block_rows

    def start(node, carry):
        wanted = wanted_ref[0, 0, node]
        block = jnp.clip(wanted, 0, blocks_here - 1)
        for group in range(groups):
            pltpu.make_async_copy(
                embedding_ref.at[block, :, pl.ds(group * LANES, LANES)],
                sent_ref.at[node, pl.ds(group * block_rows, block_rows), :],
                block_sem,
            ).start()
        labels[node] = jnp.full((LABEL_ROWS, LANES), wanted.astype(jnp.float32)).astype(jnp.bfloat16)
        return carry

    lax.fori_loop(0, node_count, start, 0, unroll=4)
    label_copy = pltpu.make_async_copy(labels, sent_ref.at[:, pl.ds(body_rows, LABEL_ROWS), :], label_sem)
    label_copy.start()
    everything = sent_ref.at[:, pl.ds(0, body_rows), :]
    pltpu.make_async_copy(everything, everything, block_sem).wait()
    label_copy.wait()


def three_terms(x):
    high = x.astype(jnp.bfloat16)
    rest = x - high.astype(jnp.float32)
    middle = rest.astype(jnp.bfloat16)
    low = (rest - middle.astype(jnp.float32)).astype(jnp.bfloat16)
    return high, middle, low


def scorer(
    blocks_here,
    arrived_hbm,
    ends_hbm,
    pair_hbm,
    weight_hbm,
    bias_hbm,
    out_weight_hbm,
    score_ref,
    pooled_ref,
    arrived,
    labels,
    ends,
    pair_ref,
    weight,
    bias_ref,
    out_weight_ref,
    first_table,
    second_table,
    terms,
    offsets_near,
    offsets,
    chunk_sems,
    sems,
):
    node_count = arrived.shape[0]
    feature_width, hidden_width = weight.shape[1:]
    groups = feature_width // LANES
    block_rows = arrived.shape[1] // groups
    body_rows = groups * block_rows
    edge_total = ends.shape[1]
    parts = hidden_width // LANES
    row_total = node_count * block_rows
    chunk_blocks = 2
    chunk_count = node_count // chunk_blocks
    chunk_rows = chunk_blocks * block_rows

    def chunk_copy(chunk):
        at = pl.ds(chunk * chunk_blocks, chunk_blocks)
        return pltpu.make_async_copy(
            arrived_hbm.at[at, pl.ds(0, body_rows), :], arrived.at[at], chunk_sems.at[chunk]
        )

    label_copy = pltpu.make_async_copy(arrived_hbm.at[:, pl.ds(body_rows, LABEL_ROWS), :], labels, sems.at[0])
    ends_copy = pltpu.make_async_copy(ends_hbm, ends, sems.at[1])
    weight_copies = [pltpu.make_async_copy(weight_hbm.at[end], weight.at[end], sems.at[2 + end]) for end in range(2)]
    bias_copies = [
        pltpu.make_async_copy(bias_hbm, bias_ref.at[pl.ds(half * parts, parts)], sems.at[4 + half]) for half in range(2)
    ]
    out_weight_copies = [
        pltpu.make_async_copy(out_weight_hbm, out_weight_ref.at[pl.ds(half * parts, parts)], sems.at[6 + half])
        for half in range(2)
    ]
    pair_copy = pltpu.make_async_copy(pair_hbm, pair_ref, sems.at[8])
    offsets_copy = pltpu.make_async_copy(offsets_near, offsets, sems.at[9])

    label_copy.start()
    ends_copy.start()
    weight_copies[0].start()
    for copy in bias_copies:
        copy.start()

    def start_chunk(chunk, carry):
        chunk_copy(chunk).start()
        return carry

    lax.fori_loop(0, chunk_count, start_chunk, 0, unroll=True)
    weight_copies[1].start()
    for copy in out_weight_copies:
        copy.start()
    pair_copy.start()

    label_copy.wait()
    ends_copy.wait()
    ids = ends[...]
    target = ids >> bits(block_rows)
    source = target >> bits(blocks_here)

    def look_up(node, delivered):
        label = labels[node].astype(jnp.float32)[:2].astype(jnp.int32)
        label = jnp.concatenate([label] * (edge_total // LANES), axis=1)
        return jnp.where(source == node, label, delivered)

    delivered = lax.fori_loop(0, node_count, look_up, jnp.full(ids.shape, -1, jnp.int32), unroll=8)
    row = (source << bits(block_rows)) + (ids & (block_rows - 1))
    row = jnp.where(delivered == (target & (blocks_here - 1)), row, row_total)
    second_of_two = lax.broadcasted_iota(jnp.int32, ids.shape, 1) & 1
    offsets_near[...] = LEAD + (row - second_of_two) * parts
    offsets_copy.start()

    for copy in bias_copies:
        copy.wait()
    bias = bias_ref[...]
    absent = pl.ds(LEAD + row_total * parts, 8)
    first_table[absent, :] = bias
    second_table[absent, :] = jnp.zeros((8, LANES), jnp.float32)

    def shares_of(chunk, end):
        blocks = [arrived[chunk * chunk_blocks + block] for block in range(chunk_blocks)]
        rows = jnp.concatenate(
            [
                jnp.concatenate([block[group * block_rows : (group + 1) * block_rows] for group in range(groups)], axis=1)
                for block in blocks
            ],
            axis=0,
        )
        return jnp.dot(rows, weight[end], preferred_element_type=jnp.float32)

    def spread(chunk, part):
        return pl.ds(LEAD + chunk * (chunk_rows * parts) + part, chunk_rows, stride=parts)

    weight_copies[0].wait()

    def project_first(chunk, carry):
        chunk_copy(chunk).wait()
        shares = shares_of(chunk, 0)
        for part in range(parts):
            first_table[spread(chunk, part), :] = (
                shares[:, part * LANES : (part + 1) * LANES] + bias[part : part + 1, :]
            )
        return carry

    lax.fori_loop(0, chunk_count, project_first, 0)
    weight_copies[1].wait()
    offsets_copy.wait()

    early = lax.broadcasted_iota(jnp.int32, (8, LANES), 0) < parts

    def two_rows(table, end, edge):
        return jnp.where(
            early, table[pl.ds(offsets[end, edge], 8), :], table[pl.ds(offsets[end, edge + 1], 8), :]
        )

    def terms_at(edge):
        return pl.ds(pl.multiple_of(edge * parts, 8), 8)

    group_edges = edge_total // chunk_count

    def project_second(chunk, carry):
        shares = shares_of(chunk, 1)
        for part in range(parts):
            second_table[spread(chunk, part), :] = shares[:, part * LANES : (part + 1) * LANES]
        for pair in range(group_edges // 2):
            edge = chunk * group_edges + 2 * pair
            terms[terms_at(edge), :] = two_rows(first_table, 0, edge)
        return carry

    lax.fori_loop(0, chunk_count, project_second, 0)

    for copy in out_weight_copies:
        copy.wait()
    out_weight = 0.5 * out_weight_ref[...]
    score_edges = 128

    def score_group(step, carry):
        for pair in range(score_edges // 2):
            edge = step * score_edges + 2 * pair
            x = terms[terms_at(edge), :] + two_rows(second_table, 1, edge)
            weighted = x * out_weight
            terms[terms_at(edge), :] = weighted + weighted * jnp.tanh(x * (GELU_A + GELU_B * (x * x)))
        return carry

    lax.fori_loop(0, edge_total // score_edges, score_group, 0)

    sums = terms[pl.ds(0, edge_total, stride=parts), :]
    for part in range(1, parts):
        sums = sums + terms[pl.ds(part, edge_total, stride=parts), :]
    scores = lax.dot_general(
        jnp.ones((8, 3 * LANES), jnp.bfloat16),
        jnp.concatenate(three_terms(sums), axis=1),
        (((1,), (1,)), ((), ())),
        preferred_element_type=jnp.float32,
    )
    score_ref[...] = scores[0:1, :]

    pair_copy.wait()
    pair = pair_ref[...] & (PAIRS_ROW - 1)
    pair_rows = PAIRS_ROW // LANES
    high = lax.broadcasted_iota(jnp.int32, (pair_rows, edge_total), 0) == (pair >> bits(LANES))
    low = lax.broadcasted_iota(jnp.int32, (LANES, edge_total), 0) == (pair & (LANES - 1))
    placed = jnp.concatenate(
        [term.astype(jnp.float32) for term in three_terms(jnp.where(high, scores[:pair_rows], 0.0))], axis=0
    )
    pooled = lax.dot_general(
        placed.astype(jnp.bfloat16),
        low.astype(jnp.float32).astype(jnp.bfloat16),
        (((1,), (1,)), ((), ())),
        preferred_element_type=jnp.float32,
    )
    pooled_ref[...] = pooled[:pair_rows] + pooled[pair_rows : 2 * pair_rows] + pooled[2 * pair_rows :]


def body(embedding, send_list, edge_ends, pair_index, w_first, b_first, w_second):
    node_count = lax.axis_size("node")
    blocks_here, block_rows, feature_width = embedding.shape
    hidden_width = w_first.shape[1]
    parts = hidden_width // LANES
    body_rows = feature_width // LANES * block_rows
    edge_total = edge_ends.shape[1]
    table_rows = LEAD + node_count * block_rows * parts + 8
    anywhere = pl.BlockSpec(memory_space=pl.ANY)
    vmem = pl.BlockSpec(memory_space=pltpu.VMEM)

    sent = pl.pallas_call(
        pick,
        out_shape=jax.ShapeDtypeStruct((node_count, body_rows + LABEL_ROWS, LANES), jnp.bfloat16),
        in_specs=[pl.BlockSpec(memory_space=pltpu.SMEM), vmem],
        out_specs=anywhere,
        scratch_shapes=[
            pltpu.VMEM((node_count, LABEL_ROWS, LANES), jnp.bfloat16),
            pltpu.SemaphoreType.DMA,
            pltpu.SemaphoreType.DMA,
        ],
    )(send_list, embedding)
    arrived = lax.all_to_all(sent, "node", split_axis=0, concat_axis=0, tiled=True)

    scores, pooled = pl.pallas_call(
        functools.partial(scorer, blocks_here),
        out_shape=(
            jax.ShapeDtypeStruct((1, edge_total), jnp.float32),
            jax.ShapeDtypeStruct((PAIRS_ROW // LANES, LANES), jnp.float32),
        ),
        in_specs=[anywhere] * 6,
        out_specs=(vmem, vmem),
        scratch_shapes=[
            pltpu.VMEM((node_count, body_rows, LANES), jnp.bfloat16),
            pltpu.VMEM((node_count, LABEL_ROWS, LANES), jnp.bfloat16),
            pltpu.VMEM((2, edge_total), jnp.int32),
            pltpu.VMEM((1, edge_total), jnp.int32),
            pltpu.VMEM((2, feature_width, hidden_width), jnp.bfloat16),
            pltpu.VMEM((2 * parts, LANES), jnp.float32),
            pltpu.VMEM((2 * parts, LANES), jnp.float32),
            pltpu.VMEM((table_rows, LANES), jnp.float32),
            pltpu.VMEM((table_rows, LANES), jnp.float32),
            pltpu.VMEM((edge_total * parts, LANES), jnp.float32),
            pltpu.VMEM((2, edge_total), jnp.int32),
            pltpu.SMEM((2, edge_total), jnp.int32),
            pltpu.SemaphoreType.DMA((node_count // 2,)),
            pltpu.SemaphoreType.DMA((10,)),
        ],
        compiler_params=pltpu.CompilerParams(vmem_limit_bytes=56 * 2**20),
    )(
        arrived,
        edge_ends,
        pair_index.reshape(1, edge_total),
        w_first.reshape(2, feature_width, hidden_width),
        b_first.reshape(parts, LANES),
        w_second.astype(jnp.float32).reshape(parts, LANES),
    )
    edge_score = scores.reshape(edge_total)
    pooled = pooled.reshape(PAIRS_ROW)
    if lax.axis_size("edge") == 2:
        mine = PAIRS_ROW // 2
        whole = pooled + lax.ppermute(pooled, "edge", [(0, 1), (1, 0)])
        pair_cost = lax.dynamic_slice(whole, (lax.axis_index("edge") * mine,), (mine,))
    else:
        pair_cost = lax.psum_scatter(pooled, "edge", scatter_dimension=0, tiled=True)
    return (edge_score, pair_cost)


def solution(mesh):
    return jax.shard_map(
        body,
        mesh=mesh,
        in_specs=(
            P("node", None, None),
            P("edge", "node", None),
            P(None, ("node", "edge")),
            P(("node", "edge")),
            P(),
            P(),
            P(),
        ),
        out_specs=(P(("node", "edge")), P(("node", "edge"))),
        check_vma=False,
    )
```

```python
import functools

import jax
import jax.numpy as jnp
from jax import lax
from jax.experimental import pallas as pl
from jax.experimental.pallas import tpu as pltpu
from jax.sharding import PartitionSpec as P

PAIRS_ROW = 1024
LANES = 128
LEAD = 8
LABEL_ROWS = 8
CHUNK_BLOCKS = 8
GELU_A = 0.7978845608028654
GELU_B = GELU_A * 0.044715


def bits(power_of_two):
    return power_of_two.bit_length() - 1


def pick(wanted_ref, embedding_ref, sent_ref, labels, block_sem, label_sem):
    node_count = sent_ref.shape[0]
    blocks_here, block_rows, feature_width = embedding_ref.shape
    groups = feature_width // LANES
    body_rows = groups * block_rows

    def start(node, carry):
        wanted = wanted_ref[0, 0, node]
        block = jnp.clip(wanted, 0, blocks_here - 1)
        for group in range(groups):
            pltpu.make_async_copy(
                embedding_ref.at[block, :, pl.ds(group * LANES, LANES)],
                sent_ref.at[node, pl.ds(group * block_rows, block_rows), :],
                block_sem,
            ).start()
        labels[node] = jnp.full((LABEL_ROWS, LANES), wanted.astype(jnp.float32)).astype(jnp.bfloat16)
        return carry

    lax.fori_loop(0, node_count, start, 0, unroll=4)
    label_copy = pltpu.make_async_copy(labels, sent_ref.at[:, pl.ds(body_rows, LABEL_ROWS), :], label_sem)
    label_copy.start()
    everything = sent_ref.at[:, pl.ds(0, body_rows), :]
    pltpu.make_async_copy(everything, everything, block_sem).wait()
    label_copy.wait()


def three_terms(x):
    high = x.astype(jnp.bfloat16)
    rest = x - high.astype(jnp.float32)
    middle = rest.astype(jnp.bfloat16)
    low = (rest - middle.astype(jnp.float32)).astype(jnp.bfloat16)
    return high, middle, low


def scorer(
    blocks_here,
    paired,
    arrived_hbm,
    ends_hbm,
    pair_hbm,
    weight_hbm,
    bias_hbm,
    out_weight_hbm,
    score_ref,
    mine_ref,
    other_ref,
    arrived,
    labels,
    ends,
    pair_ref,
    weight,
    bias_ref,
    out_weight_ref,
    first_table,
    second_table,
    terms,
    offsets_near,
    offsets,
    chunk_sems,
    sems,
):
    node_count = arrived.shape[0]
    feature_width, hidden_width = weight.shape[1:]
    groups = feature_width // LANES
    block_rows = arrived.shape[1] // groups
    body_rows = groups * block_rows
    edge_total = ends.shape[1]
    parts = hidden_width // LANES
    row_total = node_count * block_rows
    chunk_count = node_count // CHUNK_BLOCKS
    chunk_rows = CHUNK_BLOCKS * block_rows

    def chunk_copy(chunk):
        at = pl.ds(chunk * CHUNK_BLOCKS, CHUNK_BLOCKS)
        return pltpu.make_async_copy(
            arrived_hbm.at[at, pl.ds(0, body_rows), :], arrived.at[at], chunk_sems.at[chunk]
        )

    label_copy = pltpu.make_async_copy(arrived_hbm.at[:, pl.ds(body_rows, LABEL_ROWS), :], labels, sems.at[0])
    ends_copy = pltpu.make_async_copy(ends_hbm, ends, sems.at[1])
    weight_copies = [pltpu.make_async_copy(weight_hbm.at[end], weight.at[end], sems.at[2 + end]) for end in range(2)]
    bias_copies = [
        pltpu.make_async_copy(bias_hbm, bias_ref.at[pl.ds(half * parts, parts)], sems.at[4 + half]) for half in range(2)
    ]
    out_weight_copies = [
        pltpu.make_async_copy(out_weight_hbm, out_weight_ref.at[pl.ds(half * parts, parts)], sems.at[6 + half])
        for half in range(2)
    ]
    pair_copy = pltpu.make_async_copy(pair_hbm, pair_ref, sems.at[8])
    offsets_copies = [pltpu.make_async_copy(offsets_near.at[end], offsets.at[pl.ds(end * edge_total, edge_total)], sems.at[9 + end]) for end in range(2)]

    label_copy.start()
    ends_copy.start()
    weight_copies[0].start()
    for copy in bias_copies:
        copy.start()

    def start_chunk(chunk, carry):
        chunk_copy(chunk).start()
        return carry

    lax.fori_loop(0, chunk_count, start_chunk, 0, unroll=True)
    weight_copies[1].start()
    for copy in out_weight_copies:
        copy.start()
    pair_copy.start()

    label_copy.wait()
    ends_copy.wait()
    ids = ends[...]
    target = ids >> bits(block_rows)
    source = target >> bits(blocks_here)

    def look_up(node, delivered):
        label = labels[node].astype(jnp.float32)[:2].astype(jnp.int32)
        label = jnp.concatenate([label] * (edge_total // LANES), axis=1)
        return jnp.where(source == node, label, delivered)

    delivered = lax.fori_loop(0, node_count, look_up, jnp.full(ids.shape, -1, jnp.int32), unroll=8)
    row = (source << bits(block_rows)) + (ids & (block_rows - 1))
    row = jnp.where(delivered == (target & (blocks_here - 1)), row, row_total)
    second_of_two = lax.broadcasted_iota(jnp.int32, ids.shape, 1) & 1
    offsets_near[...] = LEAD + (row - second_of_two) * parts
    for copy in offsets_copies:
        copy.start()

    for copy in bias_copies:
        copy.wait()
    bias = bias_ref[...]
    absent = pl.ds(LEAD + row_total * parts, 8)
    first_table[absent, :] = bias
    second_table[absent, :] = jnp.zeros((8, LANES), jnp.float32)

    for copy in weight_copies:
        copy.wait()

    def project(chunk, carry):
        chunk_copy(chunk).wait()
        blocks = [arrived[chunk * CHUNK_BLOCKS + block] for block in range(CHUNK_BLOCKS)]
        rows = jnp.concatenate(
            [
                jnp.concatenate([block[group * block_rows : (group + 1) * block_rows] for group in range(groups)], axis=1)
                for block in blocks
            ],
            axis=0,
        )
        for end, table in enumerate((first_table, second_table)):
            shares = jnp.dot(rows, weight[end], preferred_element_type=jnp.float32)
            for part in range(parts):
                share = shares[:, part * LANES : (part + 1) * LANES]
                at = pl.ds(LEAD + chunk * (chunk_rows * parts) + part, chunk_rows, stride=parts)
                table[at, :] = share + bias[part : part + 1, :] if end == 0 else share
        return carry

    lax.fori_loop(0, chunk_count, project, 0)
    for copy in offsets_copies:
        copy.wait()

    early = lax.broadcasted_iota(jnp.int32, (8, LANES), 0) < parts

    def two_rows(table, end, edge):
        return jnp.where(
            early, table[pl.ds(offsets[end * edge_total + edge], 8), :], table[pl.ds(offsets[end * edge_total + edge + 1], 8), :]
        )

    def terms_at(edge):
        return pl.ds(pl.multiple_of(edge * parts, 8), 8)

    for copy in out_weight_copies:
        copy.wait()
    out_weight = 0.5 * out_weight_ref[...]
    score_edges = 128

    def score_group(step, carry):
        for pair in range(score_edges // 2):
            edge = step * score_edges + 2 * pair
            x = two_rows(first_table, 0, edge) + two_rows(second_table, 1, edge)
            weighted = x * out_weight
            terms[terms_at(edge), :] = weighted + weighted * jnp.tanh(x * (GELU_A + GELU_B * (x * x)))
        return carry

    lax.fori_loop(0, edge_total // score_edges, score_group, 0)

    sums = terms[pl.ds(0, edge_total, stride=parts), :]
    for part in range(1, parts):
        sums = sums + terms[pl.ds(part, edge_total, stride=parts), :]
    scores = lax.dot_general(
        jnp.ones((8, 3 * LANES), jnp.bfloat16),
        jnp.concatenate(three_terms(sums), axis=1),
        (((1,), (1,)), ((), ())),
        preferred_element_type=jnp.float32,
    )
    score_ref[...] = scores[0:1, :]

    pair_copy.wait()
    pair = pair_ref[...] & (PAIRS_ROW - 1)
    pair_rows = PAIRS_ROW // LANES
    high = lax.broadcasted_iota(jnp.int32, (pair_rows, edge_total), 0) == (pair >> bits(LANES))
    low = lax.broadcasted_iota(jnp.int32, (LANES, edge_total), 0) == (pair & (LANES - 1))
    placed = jnp.concatenate(
        [term.astype(jnp.float32) for term in three_terms(jnp.where(high, scores[:pair_rows], 0.0))], axis=0
    )
    pooled = lax.dot_general(
        placed.astype(jnp.bfloat16),
        low.astype(jnp.float32).astype(jnp.bfloat16),
        (((1,), (1,)), ((), ())),
        preferred_element_type=jnp.float32,
    )
    pooled = pooled[:pair_rows] + pooled[pair_rows : 2 * pair_rows] + pooled[2 * pair_rows :]
    half = pair_rows // 2
    low_is_mine = True if not paired else lax.axis_index("edge") == 0
    mine_ref[...] = jnp.where(low_is_mine, pooled[:half], pooled[half:])
    other_ref[...] = jnp.where(low_is_mine, pooled[half:], pooled[:half])


def call_scorer(blocks_here, paired, arrived, ends, pair, weight, bias, out_weight):
    node_count = arrived.shape[0]
    feature_width, hidden_width = weight.shape[1:]
    parts = hidden_width // LANES
    body_rows = arrived.shape[1] - LABEL_ROWS
    block_rows = body_rows * LANES // feature_width
    edge_total = ends.shape[1]
    table_rows = LEAD + node_count * block_rows * parts + 8
    needed = (2 * table_rows + edge_total * parts) * LANES * 4
    needed += 2 * (node_count * body_rows * LANES + 2 * feature_width * hidden_width)
    anywhere = pl.BlockSpec(memory_space=pl.ANY)
    vmem = pl.BlockSpec(memory_space=pltpu.VMEM)
    return pl.pallas_call(
        functools.partial(scorer, blocks_here, paired),
        out_shape=(
            jax.ShapeDtypeStruct((1, edge_total), jnp.float32),
            jax.ShapeDtypeStruct((PAIRS_ROW // LANES // 2, LANES), jnp.float32),
            jax.ShapeDtypeStruct((PAIRS_ROW // LANES // 2, LANES), jnp.float32),
        ),
        in_specs=[anywhere] * 6,
        out_specs=(vmem, vmem, vmem),
        scratch_shapes=[
            pltpu.VMEM((node_count, body_rows, LANES), jnp.bfloat16),
            pltpu.VMEM((node_count, LABEL_ROWS, LANES), jnp.bfloat16),
            pltpu.VMEM((2, edge_total), jnp.int32),
            pltpu.VMEM((1, edge_total), jnp.int32),
            pltpu.VMEM((2, feature_width, hidden_width), jnp.bfloat16),
            pltpu.VMEM((2 * parts, LANES), jnp.float32),
            pltpu.VMEM((2 * parts, LANES), jnp.float32),
            pltpu.VMEM((table_rows, LANES), jnp.float32),
            pltpu.VMEM((table_rows, LANES), jnp.float32),
            pltpu.VMEM((edge_total * parts, LANES), jnp.float32),
            pltpu.VMEM((2, edge_total), jnp.int32),
            pltpu.SMEM((2 * edge_total,), jnp.int32),
            pltpu.SemaphoreType.DMA((node_count // CHUNK_BLOCKS,)),
            pltpu.SemaphoreType.DMA((11,)),
        ],
        compiler_params=pltpu.CompilerParams(vmem_limit_bytes=needed + 6 * 2**20),
    )(arrived, ends, pair, weight, bias, out_weight)


def body(embedding, send_list, edge_ends, pair_index, w_first, b_first, w_second):
    node_count = lax.axis_size("node")
    blocks_here, block_rows, feature_width = embedding.shape
    hidden_width = w_first.shape[1]
    parts = hidden_width // LANES
    body_rows = feature_width // LANES * block_rows
    edge_total = edge_ends.shape[1]
    anywhere = pl.BlockSpec(memory_space=pl.ANY)
    vmem = pl.BlockSpec(memory_space=pltpu.VMEM)

    sent = pl.pallas_call(
        pick,
        out_shape=jax.ShapeDtypeStruct((node_count, body_rows + LABEL_ROWS, LANES), jnp.bfloat16),
        in_specs=[pl.BlockSpec(memory_space=pltpu.SMEM), vmem],
        out_specs=anywhere,
        scratch_shapes=[
            pltpu.VMEM((node_count, LABEL_ROWS, LANES), jnp.bfloat16),
            pltpu.SemaphoreType.DMA,
            pltpu.SemaphoreType.DMA,
        ],
    )(send_list, embedding)
    arrived = lax.all_to_all(sent, "node", split_axis=0, concat_axis=0, tiled=True)

    paired = lax.axis_size("edge") == 2
    scores, mine, other = call_scorer(
        blocks_here,
        paired,
        arrived,
        edge_ends,
        pair_index.reshape(1, edge_total),
        w_first.reshape(2, feature_width, hidden_width),
        b_first.reshape(parts, LANES),
        w_second.astype(jnp.float32).reshape(parts, LANES),
    )
    edge_score = scores.reshape(edge_total)
    if paired:
        pair_cost = (mine + lax.ppermute(other, "edge", [(0, 1), (1, 0)])).reshape(PAIRS_ROW // 2)
    else:
        pooled = jnp.concatenate([mine, other]).reshape(PAIRS_ROW)
        pair_cost = lax.psum_scatter(pooled, "edge", scatter_dimension=0, tiled=True)
    return (edge_score, pair_cost)


def solution(mesh):
    return jax.shard_map(
        body,
        mesh=mesh,
        in_specs=(
            P("node", None, None),
            P("edge", "node", None),
            P(None, ("node", "edge")),
            P(("node", "edge")),
            P(),
            P(),
            P(),
        ),
        out_specs=(P(("node", "edge")), P(("node", "edge"))),
        check_vma=False,
    )
```

```python
import functools

import jax
import jax.numpy as jnp
from jax import lax
from jax.experimental import pallas as pl
from jax.experimental.pallas import tpu as pltpu
from jax.sharding import PartitionSpec as P

PAIRS_ROW = 1024
LANES = 128
LEAD = 8
LABEL_ROWS = 8
IN_FLIGHT = 5
CHUNK = 4
GELU_A = 0.7978845608028654
GELU_B = GELU_A * 0.044715


def bits(power_of_two):
    return power_of_two.bit_length() - 1


def pick(node_ref, wanted_ref, embedding_ref, *sent_refs):
    blocks_here, block_rows, feature_width = embedding_ref.shape
    groups = feature_width // LANES
    for offset, sent_ref in enumerate(sent_refs):
        wanted = wanted_ref[0, 0, node_ref[0] ^ offset]
        block = jnp.clip(wanted, 0, blocks_here - 1)
        for group in range(groups):
            sent_ref[group * block_rows : (group + 1) * block_rows, :] = embedding_ref[
                block, :, group * LANES : (group + 1) * LANES
            ]
        label = jnp.full((LABEL_ROWS, LANES), wanted.astype(jnp.float32))
        sent_ref[groups * block_rows :, :] = label.astype(jnp.bfloat16)


def project(slots, block_refs, weight_ref, bias_ref, first_table, second_table):
    feature_width, hidden_width = weight_ref.shape[1:]
    groups = feature_width // LANES
    block_rows = (block_refs[0].shape[0] - LABEL_ROWS) // groups
    parts = hidden_width // LANES
    rows = jnp.concatenate(
        [
            jnp.concatenate([ref[group * block_rows : (group + 1) * block_rows, :] for group in range(groups)], axis=1)
            for ref in block_refs
        ],
        axis=0,
    )
    for end, table in enumerate((first_table, second_table)):
        shares = jnp.dot(rows, weight_ref[end], preferred_element_type=jnp.float32)
        for part in range(parts):
            share = shares[:, part * LANES : (part + 1) * LANES]
            if end == 0:
                share = share + bias_ref[part : part + 1, :]
            for place, slot in enumerate(slots):
                at = pl.ds(LEAD + slot * block_rows * parts + part, block_rows, stride=parts)
                table[at, :] = share[place * block_rows : (place + 1) * block_rows]


def open_tables(bias, first_table, second_table):
    absent = first_table.shape[0] - bias.shape[0]
    first_table[absent:, :] = bias[...]
    second_table[absent:, :] = jnp.zeros(bias.shape, jnp.float32)


def keep(weight_ref, bias_ref, out_weight_ref, ends_ref, pair_ref, weight, bias, out_weight, ends, pair):
    weight[...] = weight_ref[...]
    parts = bias_ref.shape[0]
    for copy in range(2):
        bias[copy * parts : (copy + 1) * parts, :] = bias_ref[...]
        out_weight[copy * parts : (copy + 1) * parts, :] = 0.5 * out_weight_ref[...]
    ends[...] = ends_ref[...]
    pair[...] = pair_ref[...]


def projector(slots, opening, *refs):
    count = len(slots)
    weight, bias = refs[count : count + 2]
    first_table, second_table = refs[-2:]
    if opening:
        open_tables(bias, first_table, second_table)
    project(slots, refs[:count], weight, bias, first_table, second_table)


def three_terms(x):
    high = x.astype(jnp.bfloat16)
    rest = x - high.astype(jnp.float32)
    middle = rest.astype(jnp.bfloat16)
    low = (rest - middle.astype(jnp.float32)).astype(jnp.bfloat16)
    return high, middle, low


def scorer(landing, chunks, staged, blocks_here, paired, *refs):
    node_count = len(landing)
    block_refs, refs = dict(zip(landing, refs[:node_count])), refs[node_count:]
    node_ref, ends_ref, pair_ref, weight_ref, bias_ref, out_weight_ref = refs[:6]
    refs = refs[8:] if staged else refs[6:]
    (
        score_ref,
        mine_ref,
        other_ref,
        first_table,
        second_table,
        terms,
        offsets_near,
        offsets,
        offsets_sems,
    ) = refs
    feature_width, hidden_width = weight_ref.shape[1:]
    block_rows = (block_refs[0].shape[0] - LABEL_ROWS) * LANES // feature_width
    edge_total = ends_ref.shape[1]
    parts = hidden_width // LANES
    row_total = node_count * block_rows

    ids = ends_ref[...]
    target = ids >> bits(block_rows)
    slot_of = (target >> bits(blocks_here)) ^ node_ref[0]
    delivered = jnp.full(ids.shape, -1, jnp.int32)
    for slot, ref in block_refs.items():
        label = ref[ref.shape[0] - LABEL_ROWS :, :].astype(jnp.float32)[:2].astype(jnp.int32)
        label = jnp.concatenate([label] * (edge_total // LANES), axis=1)
        delivered = jnp.where(slot_of == slot, label, delivered)
    row = (slot_of << bits(block_rows)) + (ids & (block_rows - 1))
    row = jnp.where(delivered == (target & (blocks_here - 1)), row, row_total)
    second_of_two = lax.broadcasted_iota(jnp.int32, ids.shape, 1) & 1
    offsets_near[...] = LEAD + (row - second_of_two) * parts
    offsets_copies = [
        pltpu.make_async_copy(
            offsets_near.at[end], offsets.at[pl.ds(end * edge_total, edge_total)], offsets_sems.at[end]
        )
        for end in range(2)
    ]
    for copy in offsets_copies:
        copy.start()

    if not staged:
        open_tables(bias_ref, first_table, second_table)
    for slots in chunks:
        project(slots, [block_refs[slot] for slot in slots], weight_ref, bias_ref, first_table, second_table)

    out_weight = out_weight_ref[...]
    early = lax.broadcasted_iota(jnp.int32, (8, LANES), 0) < parts
    for copy in offsets_copies:
        copy.wait()

    def two_rows(table, end, edge):
        at = end * edge_total + edge
        return jnp.where(early, table[pl.ds(offsets[at], 8), :], table[pl.ds(offsets[at + 1], 8), :])

    group_edges = 128

    def score_group(step, carry):
        for pair in range(group_edges // 2):
            edge = step * group_edges + 2 * pair
            x = two_rows(first_table, 0, edge) + two_rows(second_table, 1, edge)
            weighted = x * out_weight
            terms[pl.ds(pl.multiple_of(edge * parts, 8), 8), :] = weighted + weighted * jnp.tanh(
                x * (GELU_A + GELU_B * (x * x))
            )
        return carry

    lax.fori_loop(0, edge_total // group_edges, score_group, 0)

    sums = terms[pl.ds(0, edge_total, stride=parts), :]
    for part in range(1, parts):
        sums = sums + terms[pl.ds(part, edge_total, stride=parts), :]
    scores = lax.dot_general(
        jnp.ones((8, 3 * LANES), jnp.bfloat16),
        jnp.concatenate(three_terms(sums), axis=1),
        (((1,), (1,)), ((), ())),
        preferred_element_type=jnp.float32,
    )
    score_ref[...] = scores[0:1, :]

    pair = pair_ref[...] & (PAIRS_ROW - 1)
    pair_rows = PAIRS_ROW // LANES
    high = lax.broadcasted_iota(jnp.int32, (pair_rows, edge_total), 0) == (pair >> bits(LANES))
    low = lax.broadcasted_iota(jnp.int32, (LANES, edge_total), 0) == (pair & (LANES - 1))
    placed = jnp.concatenate(
        [term.astype(jnp.float32) for term in three_terms(jnp.where(high, scores[:pair_rows], 0.0))], axis=0
    )
    pooled = lax.dot_general(
        placed.astype(jnp.bfloat16),
        low.astype(jnp.float32).astype(jnp.bfloat16),
        (((1,), (1,)), ((), ())),
        preferred_element_type=jnp.float32,
    )
    pooled = pooled[:pair_rows] + pooled[pair_rows : 2 * pair_rows] + pooled[2 * pair_rows :]
    half = pair_rows // 2
    low_is_mine = True if not paired else lax.axis_index("edge") == 0
    mine_ref[...] = jnp.where(low_is_mine, pooled[:half], pooled[half:])
    other_ref[...] = jnp.where(low_is_mine, pooled[half:], pooled[:half])


def offsets_in_order(node_count):
    if node_count == 16:
        return [14, 2, 15, 1, 8, 5, 12, 4, 11, 3, 9, 7, 10, 6, 13]
    half = node_count // 2
    order = []
    for place in range(half):
        order.append(half + place)
        if place + 1 < half:
            order.append(place + 1)
    return order


def body(embedding, send_list, edge_ends, pair_index, w_first, b_first, w_second):
    node_count = lax.axis_size("node")
    node_self = lax.axis_index("node").astype(jnp.int32).reshape(1)
    blocks_here, block_rows, feature_width = embedding.shape
    hidden_width = w_first.shape[1]
    parts = hidden_width // LANES
    body_rows = feature_width // LANES * block_rows
    edge_total = edge_ends.shape[1]
    table_rows = LEAD + node_count * block_rows * parts + 2 * parts
    vmem = pl.BlockSpec(memory_space=pltpu.VMEM)
    smem = pl.BlockSpec(memory_space=pltpu.SMEM)
    block = jax.ShapeDtypeStruct((body_rows + LABEL_ROWS, LANES), jnp.bfloat16)
    table = jax.ShapeDtypeStruct((table_rows, LANES), jnp.float32)
    needed = (2 * table_rows + edge_total * parts) * LANES * 4 + 4 * feature_width * hidden_width
    needed += 2 * node_count * block.shape[0] * LANES
    params = pltpu.CompilerParams(vmem_limit_bytes=needed + 6 * 2**20)

    sent = pl.pallas_call(
        pick,
        out_shape=(block,) * node_count,
        in_specs=[smem, smem, vmem],
        out_specs=(vmem,) * node_count,
        compiler_params=params,
    )(node_self, send_list, embedding)

    weight = w_first.reshape(2, feature_width, hidden_width)
    bias = b_first.reshape(parts, LANES)
    out_weight = w_second.astype(jnp.float32).reshape(parts, LANES)
    ends = edge_ends
    pair = pair_index.reshape(1, edge_total)
    shared = [weight, bias, out_weight, ends, pair]
    twice = jax.ShapeDtypeStruct((2 * parts, LANES), jnp.float32)
    shared = pl.pallas_call(
        keep,
        out_shape=[weight, twice, twice, ends, pair],
        in_specs=[vmem] * 5,
        out_specs=[vmem] * 5,
        compiler_params=params,
    )(*shared)
    weight, bias, out_weight, ends, pair = shared

    def add_to_tables(slots, tables):
        blocks = [arrived[slot] for slot in slots]
        return pl.pallas_call(
            functools.partial(projector, slots, not tables),
            out_shape=[table, table],
            in_specs=[vmem] * (len(slots) + 2 + len(tables)),
            out_specs=[vmem] * 2,
            input_output_aliases={len(slots) + 2 + end: end for end in range(len(tables))},
            compiler_params=params,
        )(*blocks, weight, bias, *tables)

    staged = 4 * table_rows * LANES * 4 < 40 * 2**20
    tables = []
    order = offsets_in_order(node_count)
    landing = [0] + order
    arrived = {0: sent[0]}
    turn = node_self
    waiting = [0]
    for place, offset in enumerate(order):
        operand = sent[offset]
        if place >= IN_FLIGHT:
            landed = order[place - IN_FLIGHT]
            operand, arrived[landed], turn = lax.optimization_barrier((operand, arrived[landed], turn))
            waiting.append(landed)
        if place == IN_FLIGHT:
            operand, turn, weight, bias, out_weight, ends, pair = lax.optimization_barrier(
                (operand, turn, weight, bias, out_weight, ends, pair)
            )
        if staged and len(waiting) == CHUNK:
            tables = add_to_tables(waiting, tables)
            operand, turn, *tables = lax.optimization_barrier((operand, turn, *tables))
            waiting = []
        arrived[offset] = lax.ppermute(operand, "node", [(node, node ^ offset) for node in range(node_count)])

    done = [] if not staged else [slot for slot in landing if slot not in waiting + order[-IN_FLIGHT:]]
    last = [slot for slot in landing if slot not in done]
    chunks = [last[start : start + CHUNK] for start in range(0, len(last), CHUNK)]
    if staged:
        chunks[-1:] = [chunks[-1][:-2], chunks[-1][-2:]]
        for slots in chunks[:-1]:
            tables = add_to_tables(slots, tables)
        chunks = chunks[-1:]

    paired = lax.axis_size("edge") == 2
    half_pool = jax.ShapeDtypeStruct((PAIRS_ROW // LANES // 2, LANES), jnp.float32)
    scores, mine, other = pl.pallas_call(
        functools.partial(scorer, landing, chunks, staged, blocks_here, paired),
        out_shape=[jax.ShapeDtypeStruct((1, edge_total), jnp.float32), half_pool, half_pool] + [table] * len(tables),
        in_specs=[vmem] * node_count + [smem] + [vmem] * (5 + len(tables)),
        out_specs=[vmem] * (3 + len(tables)),
        input_output_aliases={node_count + 6 + end: 3 + end for end in range(len(tables))},
        scratch_shapes=([] if staged else [pltpu.VMEM(table.shape, table.dtype)] * 2)
        + [
            pltpu.VMEM((edge_total * parts, LANES), jnp.float32),
            pltpu.VMEM((2, edge_total), jnp.int32),
            pltpu.SMEM((2 * edge_total,), jnp.int32),
            pltpu.SemaphoreType.DMA((2,)),
        ],
        compiler_params=params,
    )(*[arrived[slot] for slot in landing], node_self, ends, pair, weight, bias, out_weight, *tables)[:3]
    edge_score = scores.reshape(edge_total)
    if paired:
        pair_cost = (mine + lax.ppermute(other, "edge", [(0, 1), (1, 0)])).reshape(PAIRS_ROW // 2)
    else:
        pooled = jnp.concatenate([mine, other]).reshape(PAIRS_ROW)
        pair_cost = lax.psum_scatter(pooled, "edge", scatter_dimension=0, tiled=True)
    return (edge_score, pair_cost)


def solution(mesh):
    return jax.shard_map(
        body,
        mesh=mesh,
        in_specs=(
            P("node", None, None),
            P("edge", "node", None),
            P(None, ("node", "edge")),
            P(("node", "edge")),
            P(),
            P(),
            P(),
        ),
        out_specs=(P(("node", "edge")), P(("node", "edge"))),
        check_vma=False,
    )
```

```python
import functools

import jax
import jax.numpy as jnp
from jax import lax
from jax.experimental import pallas as pl
from jax.experimental.pallas import tpu as pltpu
from jax.sharding import PartitionSpec as P

PAIRS_ROW = 1024
LANES = 128
LEAD = 8
LABEL_ROWS = 8
IN_FLIGHT = 5
SORT_AT = 6
LATE = 6
CHUNK = 4
GELU_A = 0.7978845608028654
GELU_B = GELU_A * 0.044715


def bits(power_of_two):
    return power_of_two.bit_length() - 1


def pick(node_ref, wanted_ref, embedding_ref, *sent_refs):
    blocks_here, block_rows, feature_width = embedding_ref.shape
    groups = feature_width // LANES
    for offset, sent_ref in enumerate(sent_refs):
        wanted = wanted_ref[0, 0, node_ref[0] ^ offset]
        block = jnp.clip(wanted, 0, blocks_here - 1)
        for group in range(groups):
            sent_ref[group * block_rows : (group + 1) * block_rows, :] = embedding_ref[
                block, :, group * LANES : (group + 1) * LANES
            ]
        label = jnp.full((LABEL_ROWS, LANES), wanted.astype(jnp.float32))
        sent_ref[groups * block_rows :, :] = label.astype(jnp.bfloat16)


def project(slots, block_refs, weight_ref, first_table, second_table):
    feature_width, hidden_width = weight_ref.shape[1:]
    groups = feature_width // LANES
    block_rows = (block_refs[0].shape[0] - LABEL_ROWS) // groups
    parts = hidden_width // LANES
    rows = jnp.concatenate(
        [
            jnp.concatenate([ref[group * block_rows : (group + 1) * block_rows, :] for group in range(groups)], axis=1)
            for ref in block_refs
        ],
        axis=0,
    )
    for end, table in enumerate((first_table, second_table)):
        shares = jnp.dot(rows, weight_ref[end], preferred_element_type=jnp.float32)
        for part in range(parts):
            share = shares[:, part * LANES : (part + 1) * LANES]
            for place, slot in enumerate(slots):
                at = pl.ds(LEAD + slot * block_rows * parts + part, block_rows, stride=parts)
                table[at, :] = share[place * block_rows : (place + 1) * block_rows]


def open_tables(parts, *tables):
    for table in tables:
        table[table.shape[0] - 2 * parts :, :] = jnp.zeros((2 * parts, LANES), jnp.float32)


def keep_weight(weight_ref, weight):
    weight[...] = weight_ref[...]


def projector(slots, opening, *refs):
    count = len(slots)
    first_table, second_table = refs[-2:]
    if opening:
        open_tables(refs[count].shape[2] // LANES, first_table, second_table)
    project(slots, refs[:count], refs[count], first_table, second_table)


def three_terms(x):
    high = x.astype(jnp.bfloat16)
    rest = x - high.astype(jnp.float32)
    middle = rest.astype(jnp.bfloat16)
    low = (rest - middle.astype(jnp.float32)).astype(jnp.bfloat16)
    return high, middle, low


def one_hot(count, places):
    return lax.broadcasted_iota(jnp.int32, (count, places.shape[1]), 0) == places


def summed_by(rows, columns, row_count):
    def sums(values):
        kept = [jnp.where(one_hot(row_count, rows), value, 0.0) for value in values]
        return lax.dot_general(
            jnp.concatenate(kept, axis=0).astype(jnp.bfloat16),
            one_hot(LANES, columns).astype(jnp.float32).astype(jnp.bfloat16),
            (((1,), (1,)), ((), ())),
            preferred_element_type=jnp.float32,
        )

    return sums


def sorter(late_slots, block_rows, blocks_here, node_ref, edges_ref, ends_out, pair_out, edge_out, late_out):
    edge_total = edges_ref.shape[1]
    groups = edge_total // LANES

    def as_rows(line):
        return jnp.concatenate([line[:, group * LANES : (group + 1) * LANES] for group in range(groups)], axis=0)

    def as_line(rows):
        return jnp.concatenate([rows[group : group + 1] for group in range(groups)], axis=1)

    ids = edges_ref[0:2, :]
    slot_of = (ids >> bits(block_rows * blocks_here)) ^ node_ref[0]
    late = jnp.zeros(ids.shape, jnp.float32)
    for slot in late_slots:
        late = jnp.where(slot_of == slot, 1.0, late)
    flags = as_rows(jnp.maximum(late[0:1], late[1:2]))

    def matrix(rows, columns, keep):
        at = [lax.broadcasted_iota(jnp.int32, (rows, columns), axis) for axis in range(2)]
        return jnp.where(keep(*at), 1.0, 0.0).astype(jnp.bfloat16)

    def product(left, right):
        return jnp.dot(left, right, preferred_element_type=jnp.float32)

    in_row = product(flags.astype(jnp.bfloat16), matrix(LANES, LANES, lambda i, j: i < j))
    of_row = product(flags.astype(jnp.bfloat16), matrix(LANES, LANES, lambda i, j: i >= 0)).astype(jnp.bfloat16)
    rows_before = product(matrix(groups, groups, lambda i, j: j < i), of_row)
    late_total = product(matrix(groups, groups, lambda i, j: i >= 0), of_row)
    late_out[...] = late_total[:8]

    index = lax.broadcasted_iota(jnp.int32, flags.shape, 0) * LANES + lax.broadcasted_iota(jnp.int32, flags.shape, 1)
    before = in_row + rows_before
    place = jnp.where(flags > 0.0, edge_total - late_total + before, index.astype(jnp.float32) - before)
    place = as_line(place.astype(jnp.int32))

    pair = edges_ref[2:3, :] & (PAIRS_ROW - 1)
    edge = lax.broadcasted_iota(jnp.int32, pair.shape, 1)
    pieces = []
    for line in (ids[0:1], ids[1:2], pair, edge):
        pieces += [(line >> 8).astype(jnp.float32), (line & 255).astype(jnp.float32)]
    moved = summed_by(place >> bits(LANES), place & (LANES - 1), groups)(pieces).astype(jnp.int32)
    moved = [moved[piece * groups : (piece + 1) * groups] for piece in range(len(pieces))]
    ends_out[:groups, :] = (moved[0] << 8) + moved[1]
    ends_out[groups:, :] = (moved[2] << 8) + moved[3]
    pair_out[...] = as_line((moved[4] << 8) + moved[5])
    edge_out[...] = as_line((moved[6] << 8) + moved[7])


class Gather:
    def __init__(self, block_refs, block_rows, blocks_here, row_total, parts, node_ref, ends_ref, late_ref, scratch):
        self.offsets_near, self.offsets, self.sems = scratch
        self.parts = parts
        self.groups = ends_ref.shape[0] // 2
        late_total = jnp.max(late_ref[...]).astype(jnp.int32)
        self.early_groups = (self.groups * LANES - late_total) >> bits(LANES)
        ids = ends_ref[...]
        target = ids >> bits(block_rows)
        slot_of = (target >> bits(blocks_here)) ^ node_ref[0]
        delivered = jnp.full(ids.shape, -1, jnp.int32)
        for slot, ref in block_refs.items():
            label = ref[ref.shape[0] - LABEL_ROWS :, :].astype(jnp.float32).astype(jnp.int32)
            label = jnp.concatenate([label] * (ids.shape[0] // LABEL_ROWS), axis=0)
            delivered = jnp.where(slot_of == slot, label, delivered)
        row = (slot_of << bits(block_rows)) + (ids & (block_rows - 1))
        row = jnp.where(delivered == (target & (blocks_here - 1)), row, row_total)
        second_of_two = lax.broadcasted_iota(jnp.int32, ids.shape, 1) & 1
        self.offsets_near[...] = LEAD + (row - second_of_two) * parts

    def copies(self, group):
        return [
            pltpu.make_async_copy(
                self.offsets_near.at[end * self.groups + group],
                self.offsets.at[pl.ds((end * self.groups + group) * LANES, LANES)],
                self.sems.at[end, group],
            )
            for end in range(2)
        ]

    def start(self, first, behind):
        def step(group, carry):
            for copy in self.copies(group):
                copy.start()
            return carry

        lax.fori_loop(first, behind, step, 0)

    def score(self, first, behind, tables, hidden_ref, terms):
        bias = hidden_ref[: 2 * self.parts, :]
        out_weight = hidden_ref[2 * self.parts :, :]
        early = lax.broadcasted_iota(jnp.int32, (8, LANES), 0) < self.parts

        def two_rows(end, edge):
            at = end * self.groups * LANES + edge
            table, offsets = tables[end], self.offsets
            return jnp.where(early, table[pl.ds(offsets[at], 8), :], table[pl.ds(offsets[at + 1], 8), :])

        def step(group, carry):
            for copy in self.copies(group):
                copy.wait()
            for pair in range(LANES // 2):
                edge = group * LANES + 2 * pair
                x = two_rows(0, edge) + two_rows(1, edge) + bias
                weighted = x * out_weight
                terms[pl.ds(pl.multiple_of(edge * self.parts, 8), 8), :] = weighted + weighted * jnp.tanh(
                    x * (GELU_A + GELU_B * (x * x))
                )
            return carry

        lax.fori_loop(first, behind, step, 0)


def early_scorer(slots, node_count, blocks_here, *refs):
    block_refs = dict(zip(slots, refs[: len(slots)]))
    node_ref, ends_ref, late_ref, hidden_ref = refs[len(slots) : len(slots) + 4]
    first_table, second_table, terms = refs[len(slots) + 6 : len(slots) + 9]
    parts = hidden_ref.shape[0] // 4
    block_rows = (first_table.shape[0] - LEAD - 2 * parts) // (node_count * parts)
    gather = Gather(
        block_refs, block_rows, blocks_here, node_count * block_rows, parts, node_ref, ends_ref, late_ref, refs[-3:]
    )
    gather.start(0, gather.early_groups)
    gather.score(0, gather.early_groups, (first_table, second_table), hidden_ref, terms)


def scorer(landing, chunks, staged, blocks_here, paired, *refs):
    node_count = len(landing)
    block_refs, refs = dict(zip(landing, refs[:node_count])), refs[node_count:]
    node_ref, ends_ref, pair_ref, edge_ref, late_ref, weight_ref, hidden_ref = refs[:7]
    refs = refs[10:] if staged else refs[7:]
    score_ref, mine_ref, other_ref, first_table, second_table, terms = refs[:6]
    feature_width, hidden_width = weight_ref.shape[1:]
    block_rows = (block_refs[0].shape[0] - LABEL_ROWS) * LANES // feature_width
    parts = hidden_width // LANES
    groups = ends_ref.shape[0] // 2
    edge_total = groups * LANES

    gather = Gather(
        block_refs, block_rows, blocks_here, node_count * block_rows, parts, node_ref, ends_ref, late_ref, refs[6:]
    )
    gather.start(gather.early_groups, groups)
    if not staged:
        open_tables(parts, first_table, second_table)
    for slots in chunks:
        project(slots, [block_refs[slot] for slot in slots], weight_ref, first_table, second_table)
    gather.score(gather.early_groups, groups, (first_table, second_table), hidden_ref, terms)

    sums = terms[pl.ds(0, edge_total, stride=parts), :]
    for part in range(1, parts):
        sums = sums + terms[pl.ds(part, edge_total, stride=parts), :]
    scores = lax.dot_general(
        jnp.full((8, 3 * LANES), 0.5, jnp.bfloat16),
        jnp.concatenate(three_terms(sums), axis=1),
        (((1,), (1,)), ((), ())),
        preferred_element_type=jnp.float32,
    )
    scores = [term.astype(jnp.float32) for term in three_terms(scores[0:1])]

    def place(rows, columns, row_count):
        sums = summed_by(rows, columns, row_count)(scores)
        return sums[:row_count] + sums[row_count : 2 * row_count] + sums[2 * row_count :]

    edge = edge_ref[...]
    score_ref[...] = place(edge >> bits(LANES), edge & (LANES - 1), groups)
    pair = pair_ref[...]
    pooled = place(pair >> bits(LANES), pair & (LANES - 1), PAIRS_ROW // LANES)
    half = PAIRS_ROW // LANES // 2
    low_is_mine = True if not paired else lax.axis_index("edge") == 0
    mine_ref[...] = jnp.where(low_is_mine, pooled[:half], pooled[half:])
    other_ref[...] = jnp.where(low_is_mine, pooled[half:], pooled[:half])


def offsets_in_order(node_count):
    if node_count == 16:
        return [2, 14, 1, 15, 5, 8, 4, 12, 3, 11, 7, 9, 6, 10, 13]
    half = node_count // 2
    order = []
    for place in range(half):
        order.append(half + place)
        if place + 1 < half:
            order.append(place + 1)
    return order


def nothing(*refs):
    pass


def after(array, others, params):
    vmem = pl.BlockSpec(memory_space=pltpu.VMEM)
    return pl.pallas_call(
        nothing,
        out_shape=jax.ShapeDtypeStruct(array.shape, array.dtype),
        in_specs=[vmem] * (1 + len(others)),
        out_specs=vmem,
        input_output_aliases={0: 0},
        compiler_params=params,
    )(array, *others)


def body(embedding, send_list, edge_ends, pair_index, w_first, b_first, w_second):
    node_count = lax.axis_size("node")
    node_self = lax.axis_index("node").astype(jnp.int32).reshape(1)
    blocks_here, block_rows, feature_width = embedding.shape
    hidden_width = w_first.shape[1]
    parts = hidden_width // LANES
    body_rows = feature_width // LANES * block_rows
    edge_total = edge_ends.shape[1]
    table_rows = LEAD + node_count * block_rows * parts + 2 * parts
    vmem = pl.BlockSpec(memory_space=pltpu.VMEM)
    smem = pl.BlockSpec(memory_space=pltpu.SMEM)
    block = jax.ShapeDtypeStruct((body_rows + LABEL_ROWS, LANES), jnp.bfloat16)
    table = jax.ShapeDtypeStruct((table_rows, LANES), jnp.float32)
    needed = (2 * table_rows + edge_total * parts) * LANES * 4 + 4 * feature_width * hidden_width
    needed += 2 * node_count * block.shape[0] * LANES
    params = pltpu.CompilerParams(vmem_limit_bytes=needed + 6 * 2**20)

    sent = pl.pallas_call(
        pick,
        out_shape=(block,) * node_count,
        in_specs=[smem, smem, vmem],
        out_specs=(vmem,) * node_count,
        compiler_params=params,
    )(node_self, send_list, embedding)

    weight = w_first.reshape(2, feature_width, hidden_width)
    bias = b_first.reshape(parts, LANES)
    out_weight = w_second.astype(jnp.float32).reshape(parts, LANES)
    hidden = jnp.concatenate([bias, bias, out_weight, out_weight])
    edges = jnp.concatenate([edge_ends, pair_index.reshape(1, edge_total)])
    weight = pl.pallas_call(
        keep_weight, out_shape=weight, in_specs=[vmem], out_specs=vmem, compiler_params=params
    )(weight)
    def add_to_tables(slots, tables):
        blocks = [arrived[slot] for slot in slots]
        return pl.pallas_call(
            functools.partial(projector, slots, not tables),
            out_shape=[table, table],
            in_specs=[vmem] * (len(slots) + 1 + len(tables)),
            out_specs=[vmem] * 2,
            input_output_aliases={len(slots) + 1 + end: end for end in range(len(tables))},
            compiler_params=params,
        )(*blocks, weight, *tables)

    staged = 4 * table_rows * LANES * 4 < 40 * 2**20
    order = offsets_in_order(node_count)
    landing = [0] + order
    early_slots = landing[:-LATE] if staged else []
    late_slots = landing[-LATE:] if staged else landing

    groups = edge_total // LANES
    sorted_edges = pl.pallas_call(
        functools.partial(sorter, late_slots, block_rows, blocks_here),
        out_shape=[
            jax.ShapeDtypeStruct((2 * groups, LANES), jnp.int32),
            jax.ShapeDtypeStruct((1, edge_total), jnp.int32),
            jax.ShapeDtypeStruct((1, edge_total), jnp.int32),
            jax.ShapeDtypeStruct((8, LANES), jnp.float32),
        ],
        in_specs=[smem, vmem],
        out_specs=[vmem] * 4,
        compiler_params=params,
    )(node_self, edges)
    ends, pair, edge, late = sorted_edges
    gather_scratch = [
        pltpu.VMEM((2 * groups, LANES), jnp.int32),
        pltpu.SMEM((2 * edge_total,), jnp.int32),
        pltpu.SemaphoreType.DMA((2, groups)),
    ]
    terms_shape = jax.ShapeDtypeStruct((edge_total * parts, LANES), jnp.float32)

    def score_early(tables):
        count = len(early_slots)
        return pl.pallas_call(
            functools.partial(early_scorer, early_slots, node_count, blocks_here),
            out_shape=[table, table, terms_shape],
            in_specs=[vmem] * count + [smem] + [vmem] * 5,
            out_specs=[vmem] * 3,
            input_output_aliases={count + 4 + end: end for end in range(2)},
            scratch_shapes=gather_scratch,
            compiler_params=params,
        )(*[arrived[slot] for slot in early_slots], node_self, ends, late, hidden, *tables)

    arrived = {0: sent[0]}
    waiting = [0]
    behind = []
    tables = []
    terms = []
    for place, offset in enumerate(order):
        operand = sent[offset]
        if place >= IN_FLIGHT:
            landed = order[place - IN_FLIGHT]
            behind = behind + [arrived[landed]]
            if place == IN_FLIGHT:
                behind = behind + [weight]
            if place == SORT_AT:
                behind = behind + [ends]
            if staged and (len(waiting) == CHUNK or waiting[-1:] == early_slots[-1:]):
                tables = add_to_tables(waiting, tables)
                if waiting[-1] == early_slots[-1]:
                    *tables, scored = score_early(tables)
                    terms = [scored]
                    behind = behind + [scored]
                behind = behind + [tables[0]]
                waiting = []
            operand = after(operand, behind, params)
            behind = [operand]
            waiting.append(landed)
        arrived[offset] = lax.ppermute(operand, "node", [(node, node ^ offset) for node in range(node_count)])

    last = (waiting + order[-IN_FLIGHT:]) if staged else landing
    chunks = [last[start : start + CHUNK] for start in range(0, len(last), CHUNK)]
    if staged:
        chunks = [last[:-2], last[-2:]]
        for slots in chunks[:-1]:
            tables = add_to_tables(slots, tables)
        chunks = chunks[-1:]

    paired = lax.axis_size("edge") == 2
    half_pool = jax.ShapeDtypeStruct((PAIRS_ROW // LANES // 2, LANES), jnp.float32)
    passed = [*tables, *terms]
    scores, mine, other = pl.pallas_call(
        functools.partial(scorer, landing, chunks, staged, blocks_here, paired),
        out_shape=[jax.ShapeDtypeStruct((groups, LANES), jnp.float32), half_pool, half_pool]
        + [jax.ShapeDtypeStruct(array.shape, array.dtype) for array in passed],
        in_specs=[vmem] * node_count + [smem] + [vmem] * (6 + len(passed)),
        out_specs=[vmem] * (3 + len(passed)),
        input_output_aliases={node_count + 7 + item: 3 + item for item in range(len(passed))},
        scratch_shapes=([] if staged else [pltpu.VMEM(kind.shape, kind.dtype) for kind in (table, table, terms_shape)])
        + gather_scratch,
        compiler_params=params,
    )(
        *[arrived[slot] for slot in landing],
        node_self,
        ends,
        pair,
        edge,
        late,
        weight,
        hidden,
        *passed,
    )[:3]
    edge_score = scores.reshape(edge_total)
    if paired:
        pair_cost = (mine + lax.ppermute(other, "edge", [(0, 1), (1, 0)])).reshape(PAIRS_ROW // 2)
    else:
        pooled = jnp.concatenate([mine, other]).reshape(PAIRS_ROW)
        pair_cost = lax.psum_scatter(pooled, "edge", scatter_dimension=0, tiled=True)
    return (edge_score, pair_cost)


def solution(mesh):
    return jax.shard_map(
        body,
        mesh=mesh,
        in_specs=(
            P("node", None, None),
            P("edge", "node", None),
            P(None, ("node", "edge")),
            P(("node", "edge")),
            P(),
            P(),
            P(),
        ),
        out_specs=(P(("node", "edge")), P(("node", "edge"))),
        check_vma=False,
    )
```

```python
import functools

import jax
import jax.numpy as jnp
from jax import lax
from jax.experimental import pallas as pl
from jax.experimental.pallas import tpu as pltpu
from jax.sharding import PartitionSpec as P

PAIRS_ROW = 1024
LANES = 128
LEAD = 8
LABEL_ROWS = 8
IN_FLIGHT = 5
SORT_AT = 6
LATE = (6, 2)
CHUNK = 4
GELU_A = 0.7978845608028654
GELU_B = GELU_A * 0.044715


def bits(power_of_two):
    return power_of_two.bit_length() - 1


def pick(node_ref, wanted_ref, embedding_ref, *sent_refs):
    blocks_here, block_rows, feature_width = embedding_ref.shape
    groups = feature_width // LANES
    for offset, sent_ref in enumerate(sent_refs):
        wanted = wanted_ref[0, 0, node_ref[0] ^ offset]
        block = jnp.clip(wanted, 0, blocks_here - 1)
        for group in range(groups):
            sent_ref[group * block_rows : (group + 1) * block_rows, :] = embedding_ref[
                block, :, group * LANES : (group + 1) * LANES
            ]
        label = jnp.full((LABEL_ROWS, LANES), wanted.astype(jnp.float32))
        sent_ref[groups * block_rows :, :] = label.astype(jnp.bfloat16)


def project(slots, block_refs, weight_ref, first_table, second_table):
    feature_width, hidden_width = weight_ref.shape[1:]
    groups = feature_width // LANES
    block_rows = (block_refs[0].shape[0] - LABEL_ROWS) // groups
    parts = hidden_width // LANES
    rows = jnp.concatenate(
        [
            jnp.concatenate([ref[group * block_rows : (group + 1) * block_rows, :] for group in range(groups)], axis=1)
            for ref in block_refs
        ],
        axis=0,
    )
    for end, table in enumerate((first_table, second_table)):
        shares = jnp.dot(rows, weight_ref[end], preferred_element_type=jnp.float32)
        for part in range(parts):
            share = shares[:, part * LANES : (part + 1) * LANES]
            for place, slot in enumerate(slots):
                at = pl.ds(LEAD + slot * block_rows * parts + part, block_rows, stride=parts)
                table[at, :] = share[place * block_rows : (place + 1) * block_rows]


def open_tables(parts, *tables):
    for table in tables:
        table[table.shape[0] - 2 * parts :, :] = jnp.zeros((2 * parts, LANES), jnp.float32)


def keep_weight(weight_ref, weight):
    weight[...] = weight_ref[...]


def projector(slots, opening, *refs):
    count = len(slots)
    first_table, second_table = refs[-2:]
    if opening:
        open_tables(refs[count].shape[2] // LANES, first_table, second_table)
    project(slots, refs[:count], refs[count], first_table, second_table)


def three_terms(x):
    high = x.astype(jnp.bfloat16)
    rest = x - high.astype(jnp.float32)
    middle = rest.astype(jnp.bfloat16)
    low = (rest - middle.astype(jnp.float32)).astype(jnp.bfloat16)
    return high, middle, low


def one_hot(count, places):
    return lax.broadcasted_iota(jnp.int32, (count, places.shape[1]), 0) == places


def summed_by(rows, columns, row_count):
    def sums(values):
        kept = [jnp.where(one_hot(row_count, rows), value, 0.0) for value in values]
        return lax.dot_general(
            jnp.concatenate(kept, axis=0).astype(jnp.bfloat16),
            one_hot(LANES, columns).astype(jnp.float32).astype(jnp.bfloat16),
            (((1,), (1,)), ((), ())),
            preferred_element_type=jnp.float32,
        )

    return sums


def sorter(late_stages, block_rows, blocks_here, node_ref, edges_ref, ends_out, pair_out, edge_out, late_out):
    edge_total = edges_ref.shape[1]
    groups = edge_total // LANES

    def as_rows(line):
        return jnp.concatenate([line[:, group * LANES : (group + 1) * LANES] for group in range(groups)], axis=0)

    def as_line(rows):
        return jnp.concatenate([rows[group : group + 1] for group in range(groups)], axis=1)

    ids = edges_ref[0:2, :]
    slot_of = (ids >> bits(block_rows * blocks_here)) ^ node_ref[0]
    def matrix(rows, columns, keep):
        at = [lax.broadcasted_iota(jnp.int32, (rows, columns), axis) for axis in range(2)]
        return jnp.where(keep(*at), 1.0, 0.0).astype(jnp.bfloat16)

    def product(left, right):
        return jnp.dot(left, right, preferred_element_type=jnp.float32)

    index = lax.broadcasted_iota(jnp.int32, (groups, LANES), 0) * LANES
    index = index + lax.broadcasted_iota(jnp.int32, (groups, LANES), 1)
    flags = [jnp.ones((groups, LANES), jnp.float32)]
    before = [index.astype(jnp.float32)]
    total = [jnp.full((groups, LANES), float(edge_total), jnp.float32)]
    for stage, late_slots in enumerate(late_stages):
        late = jnp.zeros(ids.shape, jnp.float32)
        for slot in late_slots:
            late = jnp.where(slot_of == slot, 1.0, late)
        late = as_rows(jnp.maximum(late[0:1], late[1:2]))
        in_row = product(late.astype(jnp.bfloat16), matrix(LANES, LANES, lambda i, j: i < j))
        of_row = product(late.astype(jnp.bfloat16), matrix(LANES, LANES, lambda i, j: i >= 0)).astype(jnp.bfloat16)
        flags.append(late)
        before.append(in_row + product(matrix(groups, groups, lambda i, j: j < i), of_row))
        total.append(product(matrix(groups, groups, lambda i, j: i >= 0), of_row))
        late_out[8 * stage : 8 * stage + 8, :] = total[-1][:8]
    flags.append(jnp.zeros((groups, LANES), jnp.float32))
    before.append(flags[-1])
    place = jnp.zeros((groups, LANES), jnp.float32)
    for stage in range(len(late_stages) + 1):
        here = edge_total - total[stage] + before[stage] - before[stage + 1]
        place = place + (flags[stage] - flags[stage + 1]) * here
    place = as_line(place.astype(jnp.int32))

    pair = edges_ref[2:3, :] & (PAIRS_ROW - 1)
    edge = lax.broadcasted_iota(jnp.int32, pair.shape, 1)
    pieces = []
    for line in (ids[0:1], ids[1:2], pair, edge):
        pieces += [(line >> 8).astype(jnp.float32), (line & 255).astype(jnp.float32)]
    moved = summed_by(place >> bits(LANES), place & (LANES - 1), groups)(pieces).astype(jnp.int32)
    moved = [moved[piece * groups : (piece + 1) * groups] for piece in range(len(pieces))]
    ends_out[:groups, :] = (moved[0] << 8) + moved[1]
    ends_out[groups:, :] = (moved[2] << 8) + moved[3]
    pair_out[...] = as_line((moved[4] << 8) + moved[5])
    edge_out[...] = as_line((moved[6] << 8) + moved[7])


class Gather:
    def __init__(self, block_refs, block_rows, blocks_here, row_total, parts, node_ref, ends_ref, late_ref, scratch):
        self.offsets_near, self.offsets, self.sems = scratch
        self.parts = parts
        self.groups = ends_ref.shape[0] // 2
        self.late_ref = late_ref
        ids = ends_ref[...]
        target = ids >> bits(block_rows)
        slot_of = (target >> bits(blocks_here)) ^ node_ref[0]
        delivered = jnp.full(ids.shape, -1, jnp.int32)
        for slot, ref in block_refs.items():
            label = ref[ref.shape[0] - LABEL_ROWS :, :].astype(jnp.float32).astype(jnp.int32)
            label = jnp.concatenate([label] * (ids.shape[0] // LABEL_ROWS), axis=0)
            delivered = jnp.where(slot_of == slot, label, delivered)
        row = (slot_of << bits(block_rows)) + (ids & (block_rows - 1))
        row = jnp.where(delivered == (target & (blocks_here - 1)), row, row_total)
        second_of_two = lax.broadcasted_iota(jnp.int32, ids.shape, 1) & 1
        self.offsets_near[...] = LEAD + (row - second_of_two) * parts

    def bound(self, stage):
        late_total = jnp.max(self.late_ref[8 * stage : 8 * stage + 8, :]).astype(jnp.int32)
        return (self.groups * LANES - late_total) >> bits(LANES)

    def copies(self, group):
        return [
            pltpu.make_async_copy(
                self.offsets_near.at[end * self.groups + group],
                self.offsets.at[pl.ds((end * self.groups + group) * LANES, LANES)],
                self.sems.at[end, group],
            )
            for end in range(2)
        ]

    def start(self, first, behind):
        def step(group, carry):
            for copy in self.copies(group):
                copy.start()
            return carry

        lax.fori_loop(first, behind, step, 0)

    def score(self, first, behind, tables, hidden_ref, terms):
        bias = hidden_ref[: 2 * self.parts, :]
        out_weight = hidden_ref[2 * self.parts :, :]
        early = lax.broadcasted_iota(jnp.int32, (8, LANES), 0) < self.parts

        def two_rows(end, edge):
            at = end * self.groups * LANES + edge
            table, offsets = tables[end], self.offsets
            return jnp.where(early, table[pl.ds(offsets[at], 8), :], table[pl.ds(offsets[at + 1], 8), :])

        def step(group, carry):
            for copy in self.copies(group):
                copy.wait()
            for pair in range(LANES // 2):
                edge = group * LANES + 2 * pair
                x = two_rows(0, edge) + two_rows(1, edge) + bias
                weighted = x * out_weight
                terms[pl.ds(pl.multiple_of(edge * self.parts, 8), 8), :] = weighted + weighted * jnp.tanh(
                    x * (GELU_A + GELU_B * (x * x))
                )
            return carry

        lax.fori_loop(first, behind, step, 0)


def early_scorer(stage, slots, chunk, node_count, blocks_here, *refs):
    block_refs = dict(zip(slots, refs[: len(slots)]))
    node_ref, ends_ref, late_ref, weight_ref, hidden_ref = refs[len(slots) : len(slots) + 5]
    first_table, second_table, terms = refs[-6:-3]
    parts = hidden_ref.shape[0] // 4
    block_rows = (first_table.shape[0] - LEAD - 2 * parts) // (node_count * parts)
    gather = Gather(
        block_refs, block_rows, blocks_here, node_count * block_rows, parts, node_ref, ends_ref, late_ref, refs[-3:]
    )
    first, behind = gather.bound(stage - 1) if stage > 0 else 0, gather.bound(stage)
    gather.start(first, behind)
    project(chunk, [block_refs[slot] for slot in chunk], weight_ref, first_table, second_table)
    gather.score(first, behind, (first_table, second_table), hidden_ref, terms)


def scorer(landing, chunks, staged, blocks_here, paired, *refs):
    node_count = len(landing)
    block_refs, refs = dict(zip(landing, refs[:node_count])), refs[node_count:]
    node_ref, ends_ref, pair_ref, edge_ref, late_ref, weight_ref, hidden_ref = refs[:7]
    refs = refs[10:] if staged else refs[7:]
    score_ref, mine_ref, other_ref, first_table, second_table, terms = refs[:6]
    *gather_scratch, sorted_scores = refs[6:]
    feature_width, hidden_width = weight_ref.shape[1:]
    block_rows = (block_refs[0].shape[0] - LABEL_ROWS) * LANES // feature_width
    parts = hidden_width // LANES
    groups = ends_ref.shape[0] // 2
    edge_total = groups * LANES

    gather = Gather(
        block_refs, block_rows, blocks_here, node_count * block_rows, parts, node_ref, ends_ref, late_ref, gather_scratch
    )
    first = gather.bound(late_ref.shape[0] // 8 - 1)
    gather.start(first, groups)
    if not staged:
        open_tables(parts, first_table, second_table)
    for slots in chunks:
        project(slots, [block_refs[slot] for slot in slots], weight_ref, first_table, second_table)

    def add_up(begin, end):
        edges = end - begin
        sums = terms[pl.ds(begin * parts, edges, stride=parts), :]
        for part in range(1, parts):
            sums = sums + terms[pl.ds(begin * parts + part, edges, stride=parts), :]
        scores = lax.dot_general(
            jnp.full((8, 3 * LANES), 0.5, jnp.bfloat16),
            jnp.concatenate(three_terms(sums), axis=1),
            (((1,), (1,)), ((), ())),
            preferred_element_type=jnp.float32,
        )
        sorted_scores[:, begin:end] = scores[0:1]

    half = edge_total // 2
    if staged:
        add_up(0, half)
    gather.score(first, groups, (first_table, second_table), hidden_ref, terms)

    @pl.when(first < groups // 2)
    def _():
        add_up(0, half)

    add_up(half, edge_total)
    scores = sorted_scores[...]
    scores = [term.astype(jnp.float32) for term in three_terms(scores)]

    def place(rows, columns, row_count):
        sums = summed_by(rows, columns, row_count)(scores)
        return sums[:row_count] + sums[row_count : 2 * row_count] + sums[2 * row_count :]

    edge = edge_ref[...]
    score_ref[...] = place(edge >> bits(LANES), edge & (LANES - 1), groups)
    pair = pair_ref[...]
    pooled = place(pair >> bits(LANES), pair & (LANES - 1), PAIRS_ROW // LANES)
    half = PAIRS_ROW // LANES // 2
    low_is_mine = True if not paired else lax.axis_index("edge") == 0
    mine_ref[...] = jnp.where(low_is_mine, pooled[:half], pooled[half:])
    other_ref[...] = jnp.where(low_is_mine, pooled[half:], pooled[:half])


def emit(array_ref, out_ref):
    out_ref[...] = array_ref[...]


def offsets_in_order(node_count):
    if node_count == 16:
        return [15, 14, 1, 2, 5, 8, 4, 12, 3, 11, 9, 7, 6, 10, 13]
    half = node_count // 2
    order = []
    for place in range(half):
        order.append(half + place)
        if place + 1 < half:
            order.append(place + 1)
    return order


def nothing(*refs):
    pass


def after(array, others, params):
    vmem = pl.BlockSpec(memory_space=pltpu.VMEM)
    return pl.pallas_call(
        nothing,
        out_shape=jax.ShapeDtypeStruct(array.shape, array.dtype),
        in_specs=[vmem] * (1 + len(others)),
        out_specs=vmem,
        input_output_aliases={0: 0},
        compiler_params=params,
    )(array, *others)


def body(embedding, send_list, edge_ends, pair_index, w_first, b_first, w_second):
    node_count = lax.axis_size("node")
    node_self = lax.axis_index("node").astype(jnp.int32).reshape(1)
    blocks_here, block_rows, feature_width = embedding.shape
    hidden_width = w_first.shape[1]
    parts = hidden_width // LANES
    body_rows = feature_width // LANES * block_rows
    edge_total = edge_ends.shape[1]
    table_rows = LEAD + node_count * block_rows * parts + 2 * parts
    vmem = pl.BlockSpec(memory_space=pltpu.VMEM)
    smem = pl.BlockSpec(memory_space=pltpu.SMEM)
    block = jax.ShapeDtypeStruct((body_rows + LABEL_ROWS, LANES), jnp.bfloat16)
    table = jax.ShapeDtypeStruct((table_rows, LANES), jnp.float32)
    needed = (2 * table_rows + edge_total * parts) * LANES * 4 + 4 * feature_width * hidden_width
    needed += 2 * node_count * block.shape[0] * LANES
    params = pltpu.CompilerParams(vmem_limit_bytes=needed + 6 * 2**20)

    sent = pl.pallas_call(
        pick,
        out_shape=(block,) * node_count,
        in_specs=[smem, smem, vmem],
        out_specs=(vmem,) * node_count,
        compiler_params=params,
    )(node_self, send_list, embedding)

    weight = w_first.reshape(2, feature_width, hidden_width)
    bias = b_first.reshape(parts, LANES)
    out_weight = w_second.astype(jnp.float32).reshape(parts, LANES)
    hidden = jnp.concatenate([bias, bias, out_weight, out_weight])
    edges = jnp.concatenate([edge_ends, pair_index.reshape(1, edge_total)])
    weight = pl.pallas_call(
        keep_weight, out_shape=weight, in_specs=[vmem], out_specs=vmem, compiler_params=params
    )(weight)
    def add_to_tables(slots, tables):
        blocks = [arrived[slot] for slot in slots]
        return pl.pallas_call(
            functools.partial(projector, slots, not tables),
            out_shape=[table, table],
            in_specs=[vmem] * (len(slots) + 1 + len(tables)),
            out_specs=[vmem] * 2,
            input_output_aliases={len(slots) + 1 + end: end for end in range(len(tables))},
            compiler_params=params,
        )(*blocks, weight, *tables)

    staged = 4 * table_rows * LANES * 4 < 40 * 2**20
    order = offsets_in_order(node_count)
    landing = [0] + order
    late_stages = [landing[-count:] for count in LATE] if staged else [landing]

    groups = edge_total // LANES
    sorted_edges = pl.pallas_call(
        functools.partial(sorter, late_stages, block_rows, blocks_here),
        out_shape=[
            jax.ShapeDtypeStruct((2 * groups, LANES), jnp.int32),
            jax.ShapeDtypeStruct((1, edge_total), jnp.int32),
            jax.ShapeDtypeStruct((1, edge_total), jnp.int32),
            jax.ShapeDtypeStruct((8 * len(late_stages), LANES), jnp.float32),
        ],
        in_specs=[smem, vmem],
        out_specs=[vmem] * 4,
        compiler_params=params,
    )(node_self, edges)
    ends, pair, edge, late = sorted_edges
    gather_scratch = [
        pltpu.VMEM((2 * groups, LANES), jnp.int32),
        pltpu.SMEM((2 * edge_total,), jnp.int32),
        pltpu.SemaphoreType.DMA((2, groups)),
    ]
    terms_shape = jax.ShapeDtypeStruct((edge_total * parts, LANES), jnp.float32)

    def score_early(stage, chunk, passed):
        slots = [slot for slot in landing if slot not in late_stages[stage]]
        count = len(slots)
        return pl.pallas_call(
            functools.partial(early_scorer, stage, slots, chunk, node_count, blocks_here),
            out_shape=[table, table, terms_shape],
            in_specs=[vmem] * count + [smem] + [vmem] * (4 + len(passed)),
            out_specs=[vmem] * 3,
            input_output_aliases={count + 5 + item: item for item in range(len(passed))},
            scratch_shapes=gather_scratch,
            compiler_params=params,
        )(*[arrived[slot] for slot in slots], node_self, ends, late, weight, hidden, *passed)

    arrived = {0: sent[0]}
    waiting = [0]
    behind = []
    passed = []
    stage = 0
    for place, offset in enumerate(order):
        operand = sent[offset]
        if place >= IN_FLIGHT:
            landed = order[place - IN_FLIGHT]
            behind = behind + [arrived[landed]]
            if place == IN_FLIGHT:
                behind = behind + [weight]
            if place == SORT_AT:
                behind = behind + [ends]
            if staged and stage < len(late_stages) and waiting and waiting[-1] == landing[-LATE[stage] - 1]:
                passed = score_early(stage, waiting, passed)
                behind = behind + [passed[2]]
                stage += 1
                waiting = []
            elif staged and len(waiting) == CHUNK:
                passed = add_to_tables(waiting, passed)
                behind = behind + [passed[0]]
                waiting = []
            operand = after(operand, behind, params)
            behind = [operand]
            waiting.append(landed)
        arrived[offset] = lax.ppermute(operand, "node", [(node, node ^ offset) for node in range(node_count)])

    last = (waiting + order[-IN_FLIGHT:]) if staged else landing
    chunks = [last[start : start + CHUNK] for start in range(0, len(last), CHUNK)]
    if staged:
        chunks = [last[-2:]]
        if stage < len(late_stages):
            passed = score_early(stage, last[:-2], passed)
        else:
            passed = [*add_to_tables(last[:-2], passed[:2]), passed[2]]

    paired = lax.axis_size("edge") == 2
    half_pool = jax.ShapeDtypeStruct((PAIRS_ROW // LANES // 2, LANES), jnp.float32)
    scores, mine, other = pl.pallas_call(
        functools.partial(scorer, landing, chunks, staged, blocks_here, paired),
        out_shape=[jax.ShapeDtypeStruct((groups, LANES), jnp.float32), half_pool, half_pool]
        + [jax.ShapeDtypeStruct(array.shape, array.dtype) for array in passed],
        in_specs=[vmem] * node_count + [smem] + [vmem] * (6 + len(passed)),
        out_specs=[vmem] * (3 + len(passed)),
        input_output_aliases={node_count + 7 + item: 3 + item for item in range(len(passed))},
        scratch_shapes=([] if staged else [pltpu.VMEM(kind.shape, kind.dtype) for kind in (table, table, terms_shape)])
        + gather_scratch
        + [pltpu.VMEM((1, edge_total), jnp.float32)],
        compiler_params=params,
    )(
        *[arrived[slot] for slot in landing],
        node_self,
        ends,
        pair,
        edge,
        late,
        weight,
        hidden,
        *passed,
    )[:3]
    scores = pl.pallas_call(emit, out_shape=scores, in_specs=[vmem], out_specs=vmem, compiler_params=params)(scores)
    edge_score = scores.reshape(edge_total)
    if paired:
        pair_cost = (mine + lax.ppermute(other, "edge", [(0, 1), (1, 0)])).reshape(PAIRS_ROW // 2)
    else:
        pooled = jnp.concatenate([mine, other]).reshape(PAIRS_ROW)
        pair_cost = lax.psum_scatter(pooled, "edge", scatter_dimension=0, tiled=True)
    return (edge_score, pair_cost)


def solution(mesh):
    return jax.shard_map(
        body,
        mesh=mesh,
        in_specs=(
            P("node", None, None),
            P("edge", "node", None),
            P(None, ("node", "edge")),
            P(("node", "edge")),
            P(),
            P(),
            P(),
        ),
        out_specs=(P(("node", "edge")), P(("node", "edge"))),
        check_vma=False,
    )
```

```python
import functools

import jax
import jax.numpy as jnp
from jax import lax
from jax.experimental import pallas as pl
from jax.experimental.pallas import tpu as pltpu
from jax.sharding import PartitionSpec as P

PAIRS_ROW = 1024
LANES = 128
LEAD = 8
LABEL_ROWS = 8
IN_FLIGHT = 5
SORT_AT = 6
LATE = (6, 2, 1)
CHUNK = 4
GELU_A = 0.7978845608028654
GELU_B = GELU_A * 0.044715


def bits(power_of_two):
    return power_of_two.bit_length() - 1


def pick(node_ref, wanted_ref, embedding_ref, *sent_refs):
    blocks_here, block_rows, feature_width = embedding_ref.shape
    groups = feature_width // LANES
    for offset, sent_ref in enumerate(sent_refs):
        wanted = wanted_ref[0, 0, node_ref[0] ^ offset]
        block = jnp.clip(wanted, 0, blocks_here - 1)
        for group in range(groups):
            sent_ref[group * block_rows : (group + 1) * block_rows, :] = embedding_ref[
                block, :, group * LANES : (group + 1) * LANES
            ]
        label = jnp.full((LABEL_ROWS, LANES), wanted.astype(jnp.float32))
        sent_ref[groups * block_rows :, :] = label.astype(jnp.bfloat16)


def project(slots, block_refs, weight_ref, first_table, second_table):
    feature_width, hidden_width = weight_ref.shape[1:]
    groups = feature_width // LANES
    block_rows = (block_refs[0].shape[0] - LABEL_ROWS) // groups
    parts = hidden_width // LANES
    rows = jnp.concatenate(
        [
            jnp.concatenate([ref[group * block_rows : (group + 1) * block_rows, :] for group in range(groups)], axis=1)
            for ref in block_refs
        ],
        axis=0,
    )
    for end, table in enumerate((first_table, second_table)):
        shares = jnp.dot(rows, weight_ref[end], preferred_element_type=jnp.float32)
        for part in range(parts):
            share = shares[:, part * LANES : (part + 1) * LANES]
            for place, slot in enumerate(slots):
                at = pl.ds(LEAD + slot * block_rows * parts + part, block_rows, stride=parts)
                table[at, :] = share[place * block_rows : (place + 1) * block_rows]


def open_tables(parts, *tables):
    for table in tables:
        table[table.shape[0] - 2 * parts :, :] = jnp.zeros((2 * parts, LANES), jnp.float32)


def keep_weight(weight_ref, weight):
    weight[...] = weight_ref[...]


def projector(slots, opening, *refs):
    count = len(slots)
    first_table, second_table = refs[-2:]
    if opening:
        open_tables(refs[count].shape[2] // LANES, first_table, second_table)
    project(slots, refs[:count], refs[count], first_table, second_table)


def three_terms(x):
    high = x.astype(jnp.bfloat16)
    rest = x - high.astype(jnp.float32)
    middle = rest.astype(jnp.bfloat16)
    low = (rest - middle.astype(jnp.float32)).astype(jnp.bfloat16)
    return high, middle, low


def one_hot(count, places):
    return lax.broadcasted_iota(jnp.int32, (count, places.shape[1]), 0) == places


def summed_by(rows, columns, row_count):
    def sums(values):
        kept = [jnp.where(one_hot(row_count, rows), value, 0.0) for value in values]
        return lax.dot_general(
            jnp.concatenate(kept, axis=0).astype(jnp.bfloat16),
            one_hot(LANES, columns).astype(jnp.float32).astype(jnp.bfloat16),
            (((1,), (1,)), ((), ())),
            preferred_element_type=jnp.float32,
        )

    return sums


def sorter(late_stages, block_rows, blocks_here, node_ref, edges_ref, ends_out, pair_out, edge_out, late_out):
    edge_total = edges_ref.shape[1]
    groups = edge_total // LANES

    def as_rows(line):
        return jnp.concatenate([line[:, group * LANES : (group + 1) * LANES] for group in range(groups)], axis=0)

    def as_line(rows):
        return jnp.concatenate([rows[group : group + 1] for group in range(groups)], axis=1)

    ids = edges_ref[0:2, :]
    slot_of = (ids >> bits(block_rows * blocks_here)) ^ node_ref[0]
    def matrix(rows, columns, keep):
        at = [lax.broadcasted_iota(jnp.int32, (rows, columns), axis) for axis in range(2)]
        return jnp.where(keep(*at), 1.0, 0.0).astype(jnp.bfloat16)

    def product(left, right):
        return jnp.dot(left, right, preferred_element_type=jnp.float32)

    index = lax.broadcasted_iota(jnp.int32, (groups, LANES), 0) * LANES
    index = index + lax.broadcasted_iota(jnp.int32, (groups, LANES), 1)
    flags = [jnp.ones((groups, LANES), jnp.float32)]
    before = [index.astype(jnp.float32)]
    total = [jnp.full((groups, LANES), float(edge_total), jnp.float32)]
    for stage, late_slots in enumerate(late_stages):
        late = jnp.zeros(ids.shape, jnp.float32)
        for slot in late_slots:
            late = jnp.where(slot_of == slot, 1.0, late)
        late = as_rows(jnp.maximum(late[0:1], late[1:2]))
        in_row = product(late.astype(jnp.bfloat16), matrix(LANES, LANES, lambda i, j: i < j))
        of_row = product(late.astype(jnp.bfloat16), matrix(LANES, LANES, lambda i, j: i >= 0)).astype(jnp.bfloat16)
        flags.append(late)
        before.append(in_row + product(matrix(groups, groups, lambda i, j: j < i), of_row))
        total.append(product(matrix(groups, groups, lambda i, j: i >= 0), of_row))
        late_out[8 * stage : 8 * stage + 8, :] = total[-1][:8]
    flags.append(jnp.zeros((groups, LANES), jnp.float32))
    before.append(flags[-1])
    place = jnp.zeros((groups, LANES), jnp.float32)
    for stage in range(len(late_stages) + 1):
        here = edge_total - total[stage] + before[stage] - before[stage + 1]
        place = place + (flags[stage] - flags[stage + 1]) * here
    place = as_line(place.astype(jnp.int32))

    pair = edges_ref[2:3, :] & (PAIRS_ROW - 1)
    edge = lax.broadcasted_iota(jnp.int32, pair.shape, 1)
    pieces = []
    for line in (ids[0:1], ids[1:2], pair, edge):
        pieces += [(line >> 8).astype(jnp.float32), (line & 255).astype(jnp.float32)]
    moved = summed_by(place >> bits(LANES), place & (LANES - 1), groups)(pieces).astype(jnp.int32)
    moved = [moved[piece * groups : (piece + 1) * groups] for piece in range(len(pieces))]
    ends_out[:groups, :] = (moved[0] << 8) + moved[1]
    ends_out[groups:, :] = (moved[2] << 8) + moved[3]
    pair_out[...] = as_line((moved[4] << 8) + moved[5])
    edge_out[...] = as_line((moved[6] << 8) + moved[7])


class Gather:
    def __init__(self, block_refs, block_rows, blocks_here, row_total, parts, node_ref, ends_ref, late_ref, scratch):
        self.offsets_near, self.offsets, self.sems = scratch
        self.parts = parts
        self.groups = ends_ref.shape[0] // 2
        self.late_ref = late_ref
        ids = ends_ref[...]
        target = ids >> bits(block_rows)
        slot_of = (target >> bits(blocks_here)) ^ node_ref[0]
        delivered = jnp.full(ids.shape, -1, jnp.int32)
        for slot, ref in block_refs.items():
            label = ref[ref.shape[0] - LABEL_ROWS :, :].astype(jnp.float32).astype(jnp.int32)
            label = jnp.concatenate([label] * (ids.shape[0] // LABEL_ROWS), axis=0)
            delivered = jnp.where(slot_of == slot, label, delivered)
        row = (slot_of << bits(block_rows)) + (ids & (block_rows - 1))
        row = jnp.where(delivered == (target & (blocks_here - 1)), row, row_total)
        second_of_two = lax.broadcasted_iota(jnp.int32, ids.shape, 1) & 1
        self.offsets_near[...] = LEAD + (row - second_of_two) * parts

    def bound(self, stage):
        late_total = jnp.max(self.late_ref[8 * stage : 8 * stage + 8, :]).astype(jnp.int32)
        return (self.groups * LANES - late_total) >> bits(LANES)

    def copies(self, group):
        return [
            pltpu.make_async_copy(
                self.offsets_near.at[end * self.groups + group],
                self.offsets.at[pl.ds((end * self.groups + group) * LANES, LANES)],
                self.sems.at[end, group],
            )
            for end in range(2)
        ]

    def start(self, first, behind):
        def step(group, carry):
            for copy in self.copies(group):
                copy.start()
            return carry

        lax.fori_loop(first, behind, step, 0)

    def score(self, first, behind, tables, hidden_ref, terms):
        bias = hidden_ref[: 2 * self.parts, :]
        out_weight = hidden_ref[2 * self.parts :, :]
        early = lax.broadcasted_iota(jnp.int32, (8, LANES), 0) < self.parts

        def two_rows(end, edge):
            at = end * self.groups * LANES + edge
            table, offsets = tables[end], self.offsets
            return jnp.where(early, table[pl.ds(offsets[at], 8), :], table[pl.ds(offsets[at + 1], 8), :])

        def step(group, carry):
            for copy in self.copies(group):
                copy.wait()
            for pair in range(LANES // 2):
                edge = group * LANES + 2 * pair
                x = two_rows(0, edge) + two_rows(1, edge) + bias
                weighted = x * out_weight
                terms[pl.ds(pl.multiple_of(edge * self.parts, 8), 8), :] = weighted + weighted * jnp.tanh(
                    x * (GELU_A + GELU_B * (x * x))
                )
            return carry

        lax.fori_loop(first, behind, step, 0)


def early_scorer(stage, slots, chunk, node_count, blocks_here, *refs):
    block_refs = dict(zip(slots, refs[: len(slots)]))
    node_ref, ends_ref, late_ref, weight_ref, hidden_ref = refs[len(slots) : len(slots) + 5]
    first_table, second_table, terms = refs[-6:-3]
    parts = hidden_ref.shape[0] // 4
    block_rows = (first_table.shape[0] - LEAD - 2 * parts) // (node_count * parts)
    gather = Gather(
        block_refs, block_rows, blocks_here, node_count * block_rows, parts, node_ref, ends_ref, late_ref, refs[-3:]
    )
    first, behind = gather.bound(stage - 1) if stage > 0 else 0, gather.bound(stage)
    gather.start(first, behind)
    project(chunk, [block_refs[slot] for slot in chunk], weight_ref, first_table, second_table)
    gather.score(first, behind, (first_table, second_table), hidden_ref, terms)


def scorer(landing, chunks, staged, blocks_here, paired, *refs):
    node_count = len(landing)
    block_refs, refs = dict(zip(landing, refs[:node_count])), refs[node_count:]
    node_ref, ends_ref, pair_ref, edge_ref, late_ref, weight_ref, hidden_ref = refs[:7]
    refs = refs[10:] if staged else refs[7:]
    score_ref, mine_ref, other_ref, first_table, second_table, terms = refs[:6]
    *gather_scratch, sorted_scores = refs[6:]
    feature_width, hidden_width = weight_ref.shape[1:]
    block_rows = (block_refs[0].shape[0] - LABEL_ROWS) * LANES // feature_width
    parts = hidden_width // LANES
    groups = ends_ref.shape[0] // 2
    edge_total = groups * LANES

    gather = Gather(
        block_refs, block_rows, blocks_here, node_count * block_rows, parts, node_ref, ends_ref, late_ref, gather_scratch
    )
    first = gather.bound(late_ref.shape[0] // 8 - 1)
    gather.start(first, groups)
    if not staged:
        open_tables(parts, first_table, second_table)
    for slots in chunks:
        project(slots, [block_refs[slot] for slot in slots], weight_ref, first_table, second_table)

    def add_up(begin, end):
        edges = end - begin
        sums = terms[pl.ds(begin * parts, edges, stride=parts), :]
        for part in range(1, parts):
            sums = sums + terms[pl.ds(begin * parts + part, edges, stride=parts), :]
        scores = lax.dot_general(
            jnp.full((8, 3 * LANES), 0.5, jnp.bfloat16),
            jnp.concatenate(three_terms(sums), axis=1),
            (((1,), (1,)), ((), ())),
            preferred_element_type=jnp.float32,
        )
        sorted_scores[:, begin:end] = scores[0:1]

    half = edge_total // 2
    if staged:
        add_up(0, half)
    gather.score(first, groups, (first_table, second_table), hidden_ref, terms)

    @pl.when(first < groups // 2)
    def _():
        add_up(0, half)

    add_up(half, edge_total)
    scores = sorted_scores[...]
    scores = [term.astype(jnp.float32) for term in three_terms(scores)]

    def place(rows, columns, row_count):
        sums = summed_by(rows, columns, row_count)(scores)
        return sums[:row_count] + sums[row_count : 2 * row_count] + sums[2 * row_count :]

    edge = edge_ref[...]
    score_ref[...] = place(edge >> bits(LANES), edge & (LANES - 1), groups)
    pair = pair_ref[...]
    pooled = place(pair >> bits(LANES), pair & (LANES - 1), PAIRS_ROW // LANES)
    half = PAIRS_ROW // LANES // 2
    low_is_mine = True if not paired else lax.axis_index("edge") == 0
    mine_ref[...] = jnp.where(low_is_mine, pooled[:half], pooled[half:])
    other_ref[...] = jnp.where(low_is_mine, pooled[half:], pooled[:half])


def emit(array_ref, out_ref):
    out_ref[...] = array_ref[...]


def offsets_in_order(node_count):
    if node_count == 16:
        return [14, 15, 1, 2, 5, 8, 4, 12, 3, 11, 9, 7, 6, 10, 13]
    half = node_count // 2
    order = []
    for place in range(half):
        order.append(half + place)
        if place + 1 < half:
            order.append(place + 1)
    return order


def nothing(*refs):
    pass


def after(array, others, params):
    vmem = pl.BlockSpec(memory_space=pltpu.VMEM)
    return pl.pallas_call(
        nothing,
        out_shape=jax.ShapeDtypeStruct(array.shape, array.dtype),
        in_specs=[vmem] * (1 + len(others)),
        out_specs=vmem,
        input_output_aliases={0: 0},
        compiler_params=params,
    )(array, *others)


def body(embedding, send_list, edge_ends, pair_index, w_first, b_first, w_second):
    node_count = lax.axis_size("node")
    node_self = lax.axis_index("node").astype(jnp.int32).reshape(1)
    blocks_here, block_rows, feature_width = embedding.shape
    hidden_width = w_first.shape[1]
    parts = hidden_width // LANES
    body_rows = feature_width // LANES * block_rows
    edge_total = edge_ends.shape[1]
    table_rows = LEAD + node_count * block_rows * parts + 2 * parts
    vmem = pl.BlockSpec(memory_space=pltpu.VMEM)
    smem = pl.BlockSpec(memory_space=pltpu.SMEM)
    block = jax.ShapeDtypeStruct((body_rows + LABEL_ROWS, LANES), jnp.bfloat16)
    table = jax.ShapeDtypeStruct((table_rows, LANES), jnp.float32)
    needed = (2 * table_rows + edge_total * parts) * LANES * 4 + 4 * feature_width * hidden_width
    needed += 2 * node_count * block.shape[0] * LANES
    params = pltpu.CompilerParams(vmem_limit_bytes=needed + 6 * 2**20)

    sent = pl.pallas_call(
        pick,
        out_shape=(block,) * node_count,
        in_specs=[smem, smem, vmem],
        out_specs=(vmem,) * node_count,
        compiler_params=params,
    )(node_self, jnp.maximum(send_list, -1), embedding)

    weight = w_first.reshape(2, feature_width, hidden_width)
    bias = b_first.reshape(parts, LANES)
    out_weight = w_second.astype(jnp.float32).reshape(parts, LANES)
    hidden = jnp.concatenate([bias, bias, out_weight, out_weight])
    edges = jnp.concatenate([edge_ends, pair_index.reshape(1, edge_total)])
    weight = pl.pallas_call(
        keep_weight, out_shape=weight, in_specs=[vmem], out_specs=vmem, compiler_params=params
    )(weight)
    def add_to_tables(slots, tables):
        blocks = [arrived[slot] for slot in slots]
        return pl.pallas_call(
            functools.partial(projector, slots, not tables),
            out_shape=[table, table],
            in_specs=[vmem] * (len(slots) + 1 + len(tables)),
            out_specs=[vmem] * 2,
            input_output_aliases={len(slots) + 1 + end: end for end in range(len(tables))},
            compiler_params=params,
        )(*blocks, weight, *tables)

    staged = 4 * table_rows * LANES * 4 < 40 * 2**20
    order = offsets_in_order(node_count)
    landing = [0] + order
    late_stages = [landing[-count:] for count in LATE] if staged else [landing]

    groups = edge_total // LANES
    sorted_edges = pl.pallas_call(
        functools.partial(sorter, late_stages, block_rows, blocks_here),
        out_shape=[
            jax.ShapeDtypeStruct((2 * groups, LANES), jnp.int32),
            jax.ShapeDtypeStruct((1, edge_total), jnp.int32),
            jax.ShapeDtypeStruct((1, edge_total), jnp.int32),
            jax.ShapeDtypeStruct((8 * len(late_stages), LANES), jnp.float32),
        ],
        in_specs=[smem, vmem],
        out_specs=[vmem] * 4,
        compiler_params=params,
    )(node_self, edges)
    ends, pair, edge, late = sorted_edges
    gather_scratch = [
        pltpu.VMEM((2 * groups, LANES), jnp.int32),
        pltpu.SMEM((2 * edge_total,), jnp.int32),
        pltpu.SemaphoreType.DMA((2, groups)),
    ]
    terms_shape = jax.ShapeDtypeStruct((edge_total * parts, LANES), jnp.float32)

    def score_early(stage, chunk, passed):
        slots = [slot for slot in landing if slot not in late_stages[stage]]
        count = len(slots)
        return pl.pallas_call(
            functools.partial(early_scorer, stage, slots, chunk, node_count, blocks_here),
            out_shape=[table, table, terms_shape],
            in_specs=[vmem] * count + [smem] + [vmem] * (4 + len(passed)),
            out_specs=[vmem] * 3,
            input_output_aliases={count + 5 + item: item for item in range(len(passed))},
            scratch_shapes=gather_scratch,
            compiler_params=params,
        )(*[arrived[slot] for slot in slots], node_self, ends, late, weight, hidden, *passed)

    arrived = {0: sent[0]}
    waiting = [0]
    behind = []
    passed = []
    stage = 0
    for place, offset in enumerate(order):
        operand = sent[offset]
        if place >= IN_FLIGHT:
            landed = order[place - IN_FLIGHT]
            behind = behind + [arrived[landed]]
            if place == IN_FLIGHT + 1:
                behind = behind + [weight]
            if place == SORT_AT:
                behind = behind + [ends]
            if staged and stage < len(late_stages) and waiting and waiting[-1] == landing[-LATE[stage] - 1]:
                passed = score_early(stage, waiting, passed)
                behind = behind + [passed[2]]
                stage += 1
                waiting = []
            elif staged and len(waiting) == CHUNK:
                passed = add_to_tables(waiting, passed)
                behind = behind + [passed[0]]
                waiting = []
            operand = after(operand, behind, params)
            behind = [operand]
            waiting.append(landed)
        arrived[offset] = lax.ppermute(operand, "node", [(node, node ^ offset) for node in range(node_count)])

    last = (waiting + order[-IN_FLIGHT:]) if staged else landing
    chunks = [last[start : start + CHUNK] for start in range(0, len(last), CHUNK)]
    if staged:
        while stage < len(late_stages):
            chunk = [slot for slot in last if slot not in late_stages[stage]]
            last = late_stages[stage]
            passed = score_early(stage, chunk, passed)
            stage += 1
        chunks = [last]

    paired = lax.axis_size("edge") == 2
    half_pool = jax.ShapeDtypeStruct((PAIRS_ROW // LANES // 2, LANES), jnp.float32)
    scores, mine, other = pl.pallas_call(
        functools.partial(scorer, landing, chunks, staged, blocks_here, paired),
        out_shape=[jax.ShapeDtypeStruct((groups, LANES), jnp.float32), half_pool, half_pool]
        + [jax.ShapeDtypeStruct(array.shape, array.dtype) for array in passed],
        in_specs=[vmem] * node_count + [smem] + [vmem] * (6 + len(passed)),
        out_specs=[vmem] * (3 + len(passed)),
        input_output_aliases={node_count + 7 + item: 3 + item for item in range(len(passed))},
        scratch_shapes=([] if staged else [pltpu.VMEM(kind.shape, kind.dtype) for kind in (table, table, terms_shape)])
        + gather_scratch
        + [pltpu.VMEM((1, edge_total), jnp.float32)],
        compiler_params=params,
    )(
        *[arrived[slot] for slot in landing],
        node_self,
        ends,
        pair,
        edge,
        late,
        weight,
        hidden,
        *passed,
    )[:3]
    scores = pl.pallas_call(emit, out_shape=scores, in_specs=[vmem], out_specs=vmem, compiler_params=params)(scores)
    edge_score = scores.reshape(edge_total)
    if paired:
        pair_cost = (mine + lax.ppermute(other, "edge", [(0, 1), (1, 0)])).reshape(PAIRS_ROW // 2)
    else:
        pooled = jnp.concatenate([mine, other]).reshape(PAIRS_ROW)
        pair_cost = lax.psum_scatter(pooled, "edge", scatter_dimension=0, tiled=True)
    return (edge_score, pair_cost)


def solution(mesh):
    return jax.shard_map(
        body,
        mesh=mesh,
        in_specs=(
            P("node", None, None),
            P("edge", "node", None),
            P(None, ("node", "edge")),
            P(("node", "edge")),
            P(),
            P(),
            P(),
        ),
        out_specs=(P(("node", "edge")), P(("node", "edge"))),
        check_vma=False,
    )
```
